256 devices in a mesh: row: 16 (over y, z_lo, core), col: 16 (over x, z_hi).
Axes of the slice: x: 4, y: 4, z: 8 (z_hi: 4, z_lo: 2; z = z_hi * 2 + z_lo), core: 2. Of those that a mesh axis runs over, the one named last changes fastest.
Arguments:
- out_grad: float32 [2048, 6144], P('row', 'col'), may hold values from -1.5 to 1.5
- inputs: float32 [2048, 6144], P('row', 'col'), may hold values from -6 to 6
- pre_act: float32 [2048, 12288], P('col', 'row'), may hold values from -6 to 6
- w_in: float32 [6144, 12288], P('col', 'row'), may hold values from -0.078125 to 0.078125
- w_out: float32 [12288, 6144], P('row', 'col'), may hold values from -0.0546875 to 0.0546875
- kept: int32 [8], replicated, may hold values from 64 to 256, as said below
Outputs:
- grad_inputs: float32 [2048, 6144], P('row', 'col')
- grad_w_in: float32 [6144, 12288], P('col', 'row')
- grad_w_out: float32 [12288, 6144], P('row', 'col')
The draws below stay inside these ranges and needn't reach their ends.
Inputs may be any that keep to these rules, and one draw needn't show every extreme that they name: `kept`: at least one sample keeps all 256 of its rows.
All inputs are finite; a program needn't handle non-finite values.
Results may differ from the reference program's by a relative error of at most 0.00011.
Values sent between devices are 32-bit elements; how exact they have to be, the bound alone decides.
A program may use at most 128 MiB of HBM per device.

```python
import math
import jax
import jax.numpy as jnp
from jax import lax

D = 6144
FF = 12288
PAD = 256
TOKENS = 2048
SAMPLES = 8


def draw_kept(key, part):
    key = jax.random.fold_in(key, 7)
    key_lengths, key_full = jax.random.split(key)
    counts = jax.random.randint(key_lengths, (SAMPLES,), PAD // 4, PAD + 1, dtype=jnp.int32)
    full_index = jax.random.randint(key_full, (), 0, SAMPLES, dtype=jnp.int32)
    return jnp.where(jnp.arange(SAMPLES, dtype=jnp.int32) == full_index, PAD, counts).astype(jnp.int32)


def spiked(values, key, source, target, shards_of, factor):
    def block_of(dim):
        return (jnp.arange(values.shape[dim]) // (values.shape[dim] // shards_of)).reshape((-1,) + (1,) * (values.ndim - 1 - dim))

    one_side = jax.random.permutation(key, shards_of)[block_of(target)]
    second = (block_of(target) + shards_of // 2) % shards_of
    return jnp.where((block_of(source) == one_side) | (block_of(source) == second), factor * values, values)


def block_scale(own_key, dims, pieces, least, high):
    loudness = 1.0
    for dim, shards_of in pieces:
        heights = jax.random.uniform(jax.random.fold_in(jax.random.fold_in(own_key, 6), dim), (shards_of,), jnp.float32, least / len(pieces), high / len(pieces))
        loudness = loudness * jnp.repeat(jnp.exp(heights), dims[dim] // shards_of).reshape((-1,) + (1,) * (len(dims) - 1 - dim))
    return loudness


def gaussian(key, shape, spread, reach, cuts=(), held_as=jnp.bfloat16):
    result = spread * jax.random.normal(key, shape, jnp.float32)
    if cuts:
        result = result * block_scale(key, shape, cuts, -0.22, 0.18)
    return jnp.clip(result, -reach, reach).astype(held_as)


def gaussian_with(rng, shape, scale, most, cuts, heavy, held_as=jnp.bfloat16):
    result = scale * jax.random.normal(rng, shape, jnp.float32)
    if cuts:
        result = result * block_scale(rng, shape, cuts, -0.22, 0.18)
    return jnp.clip(spiked(result, jax.random.fold_in(rng, 3), *heavy), -most, most).astype(held_as)


def setup_inputs(seed: int = 0) -> dict:
    keys = jax.random.split(jax.random.key(seed), 7)
    out_grad = gaussian_with(keys[0], (TOKENS, D), 0.25, 1.5, ((0, 16), (1, 16)), (1, 0, 16, 2.0), jnp.float32)
    inputs = gaussian(keys[1], (TOKENS, D), 1.0, 6.0, ((0, 16), (1, 16)), jnp.float32)
    pre_act = gaussian(keys[2], (TOKENS, FF), 1.0, 6.0, ((0, 16), (1, 16)), jnp.float32)
    w_in = gaussian(keys[3], (D, FF), D ** -0.5, 0.078125, ((0, 16), (1, 16)), jnp.float32)
    w_out = gaussian(keys[4], (FF, D), FF ** -0.5, 0.0546875, ((0, 16), (1, 16)), jnp.float32)
    kept = draw_kept(jax.random.fold_in(keys[6], 71), 0)
    return {"out_grad": out_grad, "inputs": inputs, "pre_act": pre_act, "w_in": w_in, "w_out": w_out, "kept": kept}


def reference(out_grad, inputs, pre_act, w_in, w_out, kept):
    highest = lax.Precision.HIGHEST
    position = jnp.arange(TOKENS, dtype=jnp.int32)
    live_rows = (position % PAD < kept[position // PAD]).astype(jnp.float32)
    grad_rows = out_grad * live_rows[:, None]
    act_grad = jnp.dot(grad_rows, w_out.T, precision=highest, preferred_element_type=jnp.float32)
    normal_cdf = 0.5 * (1.0 + jax.scipy.special.erf(pre_act / math.sqrt(2.0)))
    density = jnp.exp(-0.5 * pre_act * pre_act) / math.sqrt(2.0 * math.pi)
    activated = pre_act * normal_cdf
    pre_grad = act_grad * (normal_cdf + pre_act * density)
    grad_w_out = jnp.dot(activated.T, grad_rows, precision=highest, preferred_element_type=jnp.float32)
    grad_inputs = jnp.dot(pre_grad, w_in.T, precision=highest, preferred_element_type=jnp.float32)
    grad_w_in = jnp.dot(inputs.T, pre_grad, precision=highest, preferred_element_type=jnp.float32)
    return (grad_inputs, grad_w_in, grad_w_out)
```

```python
import functools
import math

import jax
import jax.numpy as jnp
from jax import lax
from jax.experimental import pallas as pl
from jax.experimental.pallas import tpu as pltpu
from jax.sharding import PartitionSpec as P

PAD = 256
SAMPLES = 8
TOKENS = 2048
TILE = 8
SAMPLE_TILES = PAD // TILE
TILES = TOKENS // TILE
ROWS = 128
OWN = ROWS // TILE
D = 384
F = 768
LC = 256
J = F // LC
COPIES = 160
MESH = pl.DeviceIdType.MESH
F32 = jnp.float32
BF16 = jnp.bfloat16


def split(value):
    high = value.astype(BF16)
    return high, (value - high.astype(F32)).astype(BF16)


def product(left, right, dims):
    def one(a, b):
        return lax.dot_general(a, b, (dims, ((), ())), preferred_element_type=F32)

    (lh, ll), (rh, rl) = left, right
    return one(lh, rh) + (one(ll, rh) + one(lh, rl))


NT = ((1,), (1,))
NN = ((1,), (0,))


def normal_cdf(value):
    return 0.5 * (1.0 + lax.erf(value * (1.0 / math.sqrt(2.0))))


def density(value):
    return jnp.exp(-0.5 * value * value) * (1.0 / math.sqrt(2.0 * math.pi))


def kernel(
    tb,
    kept_ref, g_ref, x_ref, p_ref, win_hbm, wout_hbm,
    dx_ref, dwin_ref, dwout_ref,
    src, inv,
    g_all, x_all, p_all, part, rx1, rx2, rz1, rz2, pg,
    gp_hi, gp_lo, gt_hi, gt_lo, xt_hi, xt_lo,
    win_f, wout_f, win_hi, win_lo, wout_hi, wout_lo,
    dxp, dxs, dsib, dy1, dy2, dz, dwt, stage, rows_buf,
    send_sem, recv_sem, local_sem,
):
    bp = tb // 16
    half = bp // 2
    steps = tb // PAD
    row, col = lax.axis_index("row"), lax.axis_index("col")
    y, zl, core = row // 4, (row // 2) % 2, row % 2
    x, zh = col // 4, col % 4

    def at_row(yy, ll, cc):
        return {"row": (yy % 4) * 4 + ll * 2 + cc, "col": col}

    def at_col(xx, hh):
        return {"row": row, "col": (xx % 4) * 4 + hh % 4}

    xp, xm = at_col(x + 1, zh), at_col(x + 3, zh)
    zp, zm = at_col(x, zh + 1), at_col(x, zh + 3)
    yp, ym = at_row(y + 1, zl, core), at_row(y + 3, zl, core)
    zlp, sib = at_row(y, 1 - zl, core), at_row(y, zl, 1 - core)
    peers = (xp, xm, zp, zm, yp, ym, zlp, sib)

    barrier = pltpu.get_barrier_semaphore()
    for peer in peers:
        pl.semaphore_signal(barrier, inc=1, device_id=peer, device_id_type=MESH)

    weights = [
        pltpu.make_async_copy(wout_hbm, wout_f, local_sem.at[0]),
        pltpu.make_async_copy(win_hbm, win_f, local_sem.at[1]),
    ]
    for w in weights:
        w.start()

    started = []

    def send(source, target, peer):
        k = len(started)
        copy = pltpu.make_async_remote_copy(
            src_ref=source, dst_ref=target, send_sem=send_sem.at[k], recv_sem=recv_sem.at[k],
            device_id=peer, device_id_type=MESH,
        )
        copy.start()
        started.append(copy)
        return copy

    limit = kept_ref[row // 2] - (row % 2) * ROWS
    position = lax.broadcasted_iota(jnp.int32, (OWN, TILE, D), 0) * TILE + lax.broadcasted_iota(
        jnp.int32, (OWN, TILE, D), 1
    )
    g_all[pl.ds(row * OWN, OWN)] = jnp.where(position < limit, g_ref[...], 0.0)
    x_all[pl.ds(row * OWN, OWN)] = x_ref[...]
    p_all[pl.ds(col * OWN, OWN)] = p_ref[...]

    pl.semaphore_wait(barrier, len(peers))

    def row_gather(ref):
        def block(yy, ll, cc):
            return ref.at[pl.ds(((yy % 4) * 4 + ll * 2 + cc) * OWN, OWN)]

        def move(peer, *where):
            return send(block(*where), block(*where), peer)

        own = (y, zl, core)
        c = {"z": move(zlp, *own), "up": move(yp, *own), "down": move(ym, *own)}
        s = [move(sib, *own)]
        yield
        c["z"].wait_recv()
        other = (y, 1 - zl, core)
        c["up2"], c["down2"] = move(yp, *other), move(ym, *other)
        s.append(move(sib, *other))
        yield
        c["up"].wait_recv()
        c["far"] = move(yp, y + 3, zl, core)
        s.append(move(sib, y + 3, zl, core))
        c["down"].wait_recv()
        s.append(move(sib, y + 1, zl, core))
        yield
        c["down2"].wait_recv()
        c["far2"] = move(ym, y + 1, 1 - zl, core)
        s.append(move(sib, y + 1, 1 - zl, core))
        c["up2"].wait_recv()
        s.append(move(sib, y + 3, 1 - zl, core))
        yield
        c["far"].wait_recv()
        s.append(move(sib, y + 2, zl, core))
        c["far2"].wait_recv()
        s.append(move(sib, y + 2, 1 - zl, core))
        yield
        for copy in s:
            copy.wait_recv()
        yield

    def col_gather(block, size):
        lo, hi = (0, size // 2), (size // 2, size // 2)

        def move(peer, xx, hh, span=(0, size)):
            ref = block(xx % 4, hh % 4, *span)
            return send(ref, ref, peer)

        c = {}
        c["za"], c["zb"] = move(zp, x, zh), move(zm, x, zh)
        c["p0"], c["m0"] = move(xp, x, zh), move(xm, x, zh)
        yield
        c["za"].wait_recv()
        c["zc"] = move(zp, x, zh + 3, lo)
        c["p3"], c["m3"] = move(xp, x, zh + 3), move(xm, x, zh + 3)
        c["zb"].wait_recv()
        c["zd"] = move(zm, x, zh + 1, hi)
        c["p1"], c["m1"] = move(xp, x, zh + 1), move(xm, x, zh + 1)
        yield
        c["zc"].wait_recv()
        c["zd"].wait_recv()
        c["p2"], c["m2"] = move(xp, x, zh + 2), move(xm, x, zh + 2)
        yield
        c["p0"].wait_recv()
        c["f0"] = move(xp, x + 3, zh)
        c["m3"].wait_recv()
        c["f3"] = move(xm, x + 1, zh + 3)
        yield
        c["p1"].wait_recv()
        c["f1"] = move(xp, x + 3, zh + 1)
        c["m2"].wait_recv()
        c["f2"] = move(xm, x + 1, zh + 2)
        yield
        for name in ("m0", "m1", "p3", "p2", "f0", "f3", "f1", "f2"):
            c[name].wait_recv()
        yield

    def col_sum(j):
        def blocks(xx, first=0, count=4):
            return part.at[j, pl.ds((xx % 4) * 4 + first, count)]

        def piece(hh, start=0, count=bp):
            return part.at[j, x * 4 + hh % 4, pl.ds(start, count)]

        c = {}

        def partial(xx):
            base = pl.multiple_of((xx % 4) * (4 * bp), 4 * bp)
            span = pl.ds(base, 4 * bp)
            units = pl.ds(j * LC, LC)
            value = product(
                (gp_hi[span], gp_lo[span]), (wout_hi[units], wout_lo[units]), NT
            )
            part[j, pl.ds((xx % 4) * 4, 4)] = value.reshape(4, bp, LC)

        partial(x + 2)
        c["a"] = send(blocks(x + 2, 0, 2), rx1.at[j, 0], xp)
        c["b"] = send(blocks(x + 2, 2, 2), rx1.at[j, 1], xm)
        yield
        partial(x + 1)
        c["c"] = send(blocks(x + 1, 2, 2), rx2.at[j, 0, pl.ds(2, 2)], xp)
        partial(x + 3)
        c["d"] = send(blocks(x + 3, 0, 2), rx2.at[j, 1, pl.ds(0, 2)], xm)
        yield
        partial(x)
        yield
        c["a"].wait_recv()
        part[j, pl.ds(((x + 1) % 4) * 4, 2)] += rx1[j, 0]
        c["e"] = send(blocks(x + 1, 0, 2), rx2.at[j, 0, pl.ds(0, 2)], xp)
        c["b"].wait_recv()
        part[j, pl.ds(((x + 3) % 4) * 4 + 2, 2)] += rx1[j, 1]
        c["f"] = send(blocks(x + 3, 2, 2), rx2.at[j, 1, pl.ds(2, 2)], xm)
        yield
        for name in ("c", "d", "e", "f"):
            c[name].wait_recv()
        part[j, pl.ds(x * 4, 4)] += rx2[j, 0] + rx2[j, 1]
        c["g"] = send(piece(zh + 2, 0, half), rz1.at[j, 0], zp)
        c["h"] = send(piece(zh + 2, half, half), rz1.at[j, 1], zm)
        c["i"] = send(piece(zh + 1, half, half), rz2.at[j, 0, pl.ds(half, half)], zp)
        c["k"] = send(piece(zh + 3, 0, half), rz2.at[j, 1, pl.ds(0, half)], zm)
        yield
        c["g"].wait_recv()
        part[j, x * 4 + (zh + 1) % 4, pl.ds(0, half)] += rz1[j, 0]
        c["l"] = send(piece(zh + 1, 0, half), rz2.at[j, 0, pl.ds(0, half)], zp)
        c["h"].wait_recv()
        part[j, x * 4 + (zh + 3) % 4, pl.ds(half, half)] += rz1[j, 1]
        c["m"] = send(piece(zh + 3, half, half), rz2.at[j, 1, pl.ds(half, half)], zm)
        yield
        for name in ("i", "k", "l", "m"):
            c[name].wait_recv()
        total = part[j, x * 4 + zh] + rz2[j, 0] + rz2[j, 1]
        mine = rows_buf[:, pl.ds(j * LC, LC)]
        slope = normal_cdf(mine) + mine * density(mine)
        pg[j, pl.ds(pl.multiple_of(col * bp, bp), bp)] = total * slope
        yield

    def pg_block(j):
        def block(xx, hh, start, count):
            first = pl.multiple_of((xx * 4 + hh) * bp + start, TILE)
            return pg.at[j, pl.ds(first, count)]

        return block

    def p_block(xx, hh, start, count):
        return p_all.at[pl.ds((xx * 4 + hh) * OWN + start, count)]

    def tables():
        live = [(kept_ref[s] + (TILE - 1)) // TILE for s in range(SAMPLES)]
        ends = []
        for s in range(SAMPLES):
            ends.append(live[s] + (ends[-1] if ends else 0))

        def fill(i, carry):
            source = i
            for s in range(SAMPLES):
                source = source + jnp.where(i >= ends[s], SAMPLE_TILES - live[s], 0)
            src[i] = jnp.where(i < ends[-1], source, -1)
            return carry

        lax.fori_loop(0, tb // TILE, fill, 0)
        for s in range(SAMPLES):
            begin = ends[s] - live[s]

            def place(i, carry, s=s, begin=begin):
                inv[s * SAMPLE_TILES + i] = jnp.where(i < live[s], begin + i, -1)
                return carry

            lax.fori_loop(0, SAMPLE_TILES, place, 0)

    def fetch(ref, first, count, masked):
        width = ref.shape[-1]

        def one(i, carry):
            at = src[first + i]
            tile = ref[jnp.maximum(at, 0)]
            if masked:
                tile = jnp.where(at >= 0, tile, 0.0)
            stage[pl.ds(pl.multiple_of(i * TILE, TILE), TILE), pl.ds(0, width)] = tile
            return carry

        lax.fori_loop(0, count, one, 0, unroll=4)
        return stage[pl.ds(0, count * TILE), pl.ds(0, width)]

    def pack_g():
        def body(t, carry):
            value = fetch(g_all, t * SAMPLE_TILES, SAMPLE_TILES, True)
            span = pl.ds(pl.multiple_of(t * PAD, PAD), PAD)
            gp_hi[span], gp_lo[span] = split(value)
            return carry

        lax.fori_loop(0, steps, body, 0)

    def transposed(ref, to_hi, to_lo, masked):
        def body(t, carry):
            value = fetch(ref, t * SAMPLE_TILES, SAMPLE_TILES, masked).T
            high, low = split(value)
            to_hi[t] = high
            to_lo[t] = low
            return carry

        lax.fori_loop(0, steps, body, 0)

    def own_rows():
        def one(i, carry):
            at = src[col * (bp // TILE) + i]
            rows_buf[pl.ds(pl.multiple_of(i * TILE, TILE), TILE)] = p_all[jnp.maximum(at, 0)]
            return carry

        lax.fori_loop(0, bp // TILE, one, 0)

    def w_out_grad():
        dwt[...] = jnp.zeros_like(dwt)

        def body(t, carry):
            value = fetch(p_all, t * SAMPLE_TILES, SAMPLE_TILES, False)
            act = split(value * normal_cdf(value))
            dwt[...] += product((gt_hi[t], gt_lo[t]), act, NN)
            return carry

        lax.fori_loop(0, steps, body, 0)
        dwout_ref[...] = dwt[...].T

    def w_in_grad(j):
        units = pl.ds(j * LC, LC)

        def body(t, carry):
            value = split(pg[j, pl.ds(pl.multiple_of(t * PAD, PAD), PAD)])
            dwin_ref[:, units] += product((xt_hi[t], xt_lo[t]), value, NN)
            return carry

        lax.fori_loop(0, steps, body, 0)

    def x_grad(j):
        def body(t, carry):
            value = split(pg[j, pl.ds(pl.multiple_of(t * PAD, PAD), PAD)])
            out = product(value, (win_hi[j], win_lo[j]), NT).reshape(SAMPLE_TILES, TILE, D)
            span = pl.ds(t * SAMPLE_TILES, SAMPLE_TILES)
            if j == 0:
                dxp[span] = out
            else:
                dxp[span] += out
            return carry

        lax.fori_loop(0, steps, body, 0)

    def row_sum():
        def spread(yy, cc):
            yy = yy % 4

            def one(i, carry):
                ll = i // OWN
                at = inv[(yy * 4 + ll * 2 + cc) * OWN + i % OWN]
                tile = dxp[jnp.maximum(at, 0)]
                dxs[cc, yy, i] = jnp.where(at >= 0, tile, 0.0)
                return carry

            lax.fori_loop(0, 2 * OWN, one, 0, unroll=4)

        order = (y + 2, y + 1, y + 3, y)
        s = []
        for k, yy in enumerate(order):
            spread(yy, 1 - core)
            s.append(send(dxs.at[1 - core, yy % 4], dsib.at[k], sib))
        yield
        for yy in order:
            spread(yy, core)

        def blocks(yy, ll):
            return dxs.at[core, yy % 4, pl.ds(ll * OWN, OWN)]

        def add_sib(k):
            s[k].wait_recv()
            dxs[core, order[k] % 4] += dsib[k]

        c = {}
        add_sib(0)
        c["a"] = send(blocks(y + 2, 0), dy1.at[0], yp)
        c["b"] = send(blocks(y + 2, 1), dy1.at[1], ym)
        add_sib(1)
        c["c"] = send(blocks(y + 1, 1), dy2.at[0, pl.ds(OWN, OWN)], yp)
        add_sib(2)
        c["d"] = send(blocks(y + 3, 0), dy2.at[1, pl.ds(0, OWN)], ym)
        add_sib(3)
        yield
        c["a"].wait_recv()
        dxs[core, (y + 1) % 4, pl.ds(0, OWN)] += dy1[0]
        c["e"] = send(blocks(y + 1, 0), dy2.at[0, pl.ds(0, OWN)], yp)
        c["b"].wait_recv()
        dxs[core, (y + 3) % 4, pl.ds(OWN, OWN)] += dy1[1]
        c["f"] = send(blocks(y + 3, 1), dy2.at[1, pl.ds(OWN, OWN)], ym)
        yield
        for name in ("c", "d", "e", "f"):
            c[name].wait_recv()
        dxs[core, y] += dy2[0] + dy2[1]
        c["z"] = send(blocks(y, 1 - zl), dz, zlp)
        yield
        c["z"].wait_recv()
        dx_ref[...] = dxs[core, y, pl.ds(zl * OWN, OWN)] + dz[...]
        yield

    g_steps, x_steps = row_gather(g_all), row_gather(x_all)
    p_steps = col_gather(p_block, OWN)
    sums = [col_sum(j) for j in range(J)]
    gathers = [col_gather(pg_block(j), bp) for j in range(J)]

    def go(steps_of, count=1):
        for _ in range(count):
            next(steps_of)

    go(g_steps)
    go(p_steps)
    tables()
    weights[0].wait()
    wout_hi[...], wout_lo[...] = split(wout_f[...])
    go(g_steps, 2)
    go(p_steps)
    go(g_steps, 3)
    pack_g()
    go(sums[0], 2)
    go(p_steps)
    go(x_steps)
    go(sums[0])
    go(sums[1], 3)
    go(sums[2], 3)
    weights[1].wait()
    for j in range(J):
        win_hi[j], win_lo[j] = split(win_f[:, pl.ds(j * LC, LC)])
    go(x_steps, 2)
    go(p_steps, 2)
    go(x_steps, 3)
    transposed(g_all, gt_hi, gt_lo, True)
    dwin_ref[...] = jnp.zeros_like(dwin_ref)
    go(sums[0])
    go(sums[1])
    go(p_steps)
    own_rows()
    go(sums[0])
    go(sums[2])
    go(sums[0])
    go(sums[1])
    go(sums[0])
    go(gathers[0])
    go(sums[1])
    go(sums[2])
    go(sums[1])
    go(gathers[1])
    go(gathers[0])
    transposed(x_all, xt_hi, xt_lo, False)
    go(sums[2])
    go(gathers[0])
    go(sums[2])
    go(gathers[2])
    go(gathers[1])
    go(gathers[0], 2)
    go(gathers[1])
    go(gathers[2])
    w_out_grad()
    go(gathers[0])
    x_grad(0)
    go(gathers[2])
    go(gathers[1], 2)
    w_in_grad(0)
    go(gathers[1])
    x_grad(1)
    go(gathers[2], 2)
    w_in_grad(1)
    go(gathers[2])
    x_grad(2)
    tail = row_sum()
    go(tail, 4)
    w_in_grad(2)
    go(tail)
    for copy in started:
        copy.wait_send()
    assert len(started) <= COPIES


def grad_kernel(tb, out_grad, inputs, pre_act, w_in, w_out, kept):
    bp = tb // 16
    vmem = pl.BlockSpec(memory_space=pltpu.VMEM)
    anywhere = pl.BlockSpec(memory_space=pl.ANY)

    def room(*shape, dtype=F32):
        return pltpu.VMEM(shape, dtype)

    half = functools.partial(room, dtype=BF16)
    steps = tb // PAD
    dx, dwin, dwout = pl.pallas_call(
        functools.partial(kernel, tb),
        out_shape=(
            jax.ShapeDtypeStruct((OWN, TILE, D), F32),
            jax.ShapeDtypeStruct((D, F), F32),
            jax.ShapeDtypeStruct((F, D), F32),
        ),
        in_specs=[pl.BlockSpec(memory_space=pltpu.SMEM), vmem, vmem, vmem, anywhere, anywhere],
        out_specs=(vmem, vmem, vmem),
        scratch_shapes=[
            pltpu.SMEM((tb // TILE,), jnp.int32),
            pltpu.SMEM((TILES,), jnp.int32),
            room(TILES, TILE, D),
            room(TILES, TILE, D),
            room(TILES, TILE, F),
            room(J, 16, bp, LC),
            room(J, 2, 2, bp, LC),
            room(J, 2, 4, bp, LC),
            room(J, 2, bp // 2, LC),
            room(J, 2, bp, LC),
            room(J, tb, LC),
            half(tb, D),
            half(tb, D),
            half(steps, D, PAD),
            half(steps, D, PAD),
            half(steps, D, PAD),
            half(steps, D, PAD),
            room(D, F),
            room(F, D),
            half(J, D, LC),
            half(J, D, LC),
            half(F, D),
            half(F, D),
            room(tb // TILE, TILE, D),
            room(2, 4, 2 * OWN, TILE, D),
            room(4, 2 * OWN, TILE, D),
            room(2, OWN, TILE, D),
            room(2, 2 * OWN, TILE, D),
            room(OWN, TILE, D),
            room(D, F),
            room(PAD, F),
            room(bp, F),
            pltpu.SemaphoreType.DMA((COPIES,)),
            pltpu.SemaphoreType.DMA((COPIES,)),
            pltpu.SemaphoreType.DMA((2,)),
        ],
        compiler_params=pltpu.CompilerParams(
            collective_id=tb // PAD, has_side_effects=True, vmem_limit_bytes=64 * 1024 * 1024
        ),
        cost_estimate=pl.CostEstimate(flops=12 * tb * D * F * 2, bytes_accessed=6 * 1024 * 1024, transcendentals=0),
    )(
        kept,
        out_grad.reshape(OWN, TILE, D),
        inputs.reshape(OWN, TILE, D),
        pre_act.reshape(OWN, TILE, F),
        w_in,
        w_out,
    )
    return dx.reshape(ROWS, D), dwin, dwout


def shards(*args):
    return grad_kernel(TOKENS, *args)


def solution(mesh):
    return jax.shard_map(
        shards,
        mesh=mesh,
        in_specs=(
            P("row", "col"),
            P("row", "col"),
            P("col", "row"),
            P("col", "row"),
            P("row", "col"),
            P(),
        ),
        out_specs=(P("row", "col"), P("col", "row"), P("row", "col")),
        check_vma=False,
    )
```

```python
import functools
import math

import jax
import jax.numpy as jnp
from jax import lax
from jax.experimental import pallas as pl
from jax.experimental.pallas import tpu as pltpu
from jax.sharding import PartitionSpec as P

PAD = 256
SAMPLES = 8
TOKENS = 2048
TILE = 8
SAMPLE_TILES = PAD // TILE
TILES = TOKENS // TILE
ROWS = 128
OWN = ROWS // TILE
D = 384
F = 768
LC = 256
J = F // LC
COPIES = 176
CROSS = 8
BUCKETS = (1280, 1536, 2048)
ORDER = (
    "g", "p", "tab", "wo", "q", "x", "g", "g", "g", "p", "p", "p", "x", "x", "x", "g", "g", "q", "g", "q", "q",
    "x", "p", "g", "p", "p", "x", "q", "g", "pack", "s0", "s0", "s0", "s0", "s1", "s1", "s1", "s1", "s2", "s2",
    "s2", "s2", "p", "q", "x", "x", "wi", "s0", "s0", "gt", "x", "gt", "xt", "xt", "s1", "s1", "q", "q", "s2",
    "s2", "p", "q", "own", "dwo", "s0", "dwo", "s1", "dwo", "s0", "s0", "s2", "dwo", "s1", "s1", "dwo", "s0",
    "a0", "s2", "s2", "a0", "s1", "a1", "a0", "a0", "a1", "s2", "a2", "a1", "a1", "a0", "a0", "a0", "a2", "a2",
    "a2", "a0", "a1", "a1", "a1", "a2", "a2", "a0", "dx0", "dx0", "dx0", "a1", "a2", "dx0", "dw0", "dw0", "a2",
    "a1", "dx1", "dx1", "dx1", "a2", "dx1", "dx2", "dx2", "dx2", "dx2", "t", "t", "dw1", "t", "dw1", "t", "dw2",
    "t", "dw2", "t", "t", "t", "t", "t",
)
MESH = pl.DeviceIdType.MESH
F32 = jnp.float32
BF16 = jnp.bfloat16


def split(value):
    high = value.astype(BF16)
    return high, (value - high.astype(F32)).astype(BF16)


def product(left, right, dims):
    def one(a, b):
        return lax.dot_general(a, b, (dims, ((), ())), preferred_element_type=F32)

    (lh, ll), (rh, rl) = left, right
    return one(lh, rh) + (one(ll, rh) + one(lh, rl))


NT = ((1,), (1,))
NN = ((1,), (0,))


def normal_cdf(value):
    return 0.5 * (1.0 + lax.erf(value * (1.0 / math.sqrt(2.0))))


def density(value):
    return jnp.exp(-0.5 * value * value) * (1.0 / math.sqrt(2.0 * math.pi))


def kernel(
    tb,
    kept_ref, g_ref, x_ref, p_ref, win_hbm, wout_hbm,
    dx_ref, dwin_ref, dwout_ref,
    src, inv,
    g_all, x_all, p_all, part, rx1, rx2, rz1, rz2, pg,
    gp_hi, gp_lo, gt_hi, gt_lo, xt_hi, xt_lo,
    win_f, wout_f, win_hi, win_lo, wout_hi, wout_lo,
    dxp, dxs, dsib, dy1, dy2, dz, dwt, stage, rows_buf,
    send_sem, recv_sem, local_sem,
):
    bp = tb // 16
    half = bp // 16 * 8
    rest = bp - half
    steps = tb // PAD
    row, col = lax.axis_index("row"), lax.axis_index("col")
    y, zl, core = row // 4, (row // 2) % 2, row % 2
    x, zh = col // 4, col % 4

    def at_row(yy, ll, cc):
        return {"row": (yy % 4) * 4 + ll * 2 + cc, "col": col}

    def at_col(xx, hh):
        return {"row": row, "col": (xx % 4) * 4 + hh % 4}

    xp, xm = at_col(x + 1, zh), at_col(x + 3, zh)
    zp, zm = at_col(x, zh + 1), at_col(x, zh + 3)
    yp, ym = at_row(y + 1, zl, core), at_row(y + 3, zl, core)
    zlp, sib = at_row(y, 1 - zl, core), at_row(y, zl, 1 - core)
    peers = (xp, xm, zp, zm, yp, ym, zlp, sib)

    barrier = pltpu.get_barrier_semaphore()
    for peer in peers:
        pl.semaphore_signal(barrier, inc=1, device_id=peer, device_id_type=MESH)

    weights = [
        pltpu.make_async_copy(wout_hbm, wout_f, local_sem.at[0]),
        pltpu.make_async_copy(win_hbm, win_f, local_sem.at[1]),
    ]
    for w in weights:
        w.start()

    started = []

    def send(source, target, peer):
        k = len(started)
        copy = pltpu.make_async_remote_copy(
            src_ref=source, dst_ref=target, send_sem=send_sem.at[k], recv_sem=recv_sem.at[k],
            device_id=peer, device_id_type=MESH,
        )
        copy.start()
        started.append(copy)
        return copy

    limit = kept_ref[row // 2] - (row % 2) * ROWS
    position = lax.broadcasted_iota(jnp.int32, (OWN, TILE, D), 0) * TILE + lax.broadcasted_iota(
        jnp.int32, (OWN, TILE, D), 1
    )
    g_all[pl.ds(row * OWN, OWN)] = jnp.where(position < limit, g_ref[...], 0.0)
    x_all[pl.ds(row * OWN, OWN)] = x_ref[...]
    p_all[pl.ds(col * OWN, OWN)] = p_ref[...]

    pl.semaphore_wait(barrier, len(peers))

    def row_gather(ref):
        def block(yy, ll, cc):
            return ref.at[pl.ds(((yy % 4) * 4 + ll * 2 + cc) * OWN, OWN)]

        def move(peer, *where):
            return send(block(*where), block(*where), peer)

        own = (y, zl, core)
        c = {"z": move(zlp, *own), "up": move(yp, *own), "down": move(ym, *own)}
        s = [move(sib, *own)]
        yield
        c["z"].wait_recv()
        other = (y, 1 - zl, core)
        c["up2"], c["down2"] = move(yp, *other), move(ym, *other)
        s.append(move(sib, *other))
        yield
        c["up"].wait_recv()
        c["far"] = move(yp, y + 3, zl, core)
        s.append(move(sib, y + 3, zl, core))
        yield
        c["down"].wait_recv()
        s.append(move(sib, y + 1, zl, core))
        yield
        c["down2"].wait_recv()
        c["far2"] = move(ym, y + 1, 1 - zl, core)
        s.append(move(sib, y + 1, 1 - zl, core))
        yield
        c["up2"].wait_recv()
        s.append(move(sib, y + 3, 1 - zl, core))
        yield
        c["far"].wait_recv()
        s.append(move(sib, y + 2, zl, core))
        yield
        c["far2"].wait_recv()
        s.append(move(sib, y + 2, 1 - zl, core))
        yield
        for copy in s:
            copy.wait_recv()
        yield

    def col_gather(block, size, z_first=True):
        cut = size // 2 if size < 16 else size // 16 * TILE
        lo, hi = (0, cut), (cut, size - cut)
        u, v, ups, vps = (zh, x, (zp, zm), (xp, xm)) if z_first else (x, zh, (xp, xm), (zp, zm))

        def move(peer, uu, vv, span=(0, size)):
            xx, hh = (vv, uu) if z_first else (uu, vv)
            ref = block(xx % 4, hh % 4, *span)
            return send(ref, ref, peer)

        c = {}
        c["ua"], c["ub"] = move(ups[0], u, v), move(ups[1], u, v)
        c["p0"], c["m0"] = move(vps[0], u, v), move(vps[1], u, v)
        yield
        c["p0"].wait_recv()
        c["f0"] = move(vps[0], u, v + 3)
        yield
        c["ua"].wait_recv()
        c["uc"] = move(ups[0], u + 3, v, lo)
        c["p3"], c["m3"] = move(vps[0], u + 3, v), move(vps[1], u + 3, v)
        yield
        c["ub"].wait_recv()
        c["ud"] = move(ups[1], u + 1, v, hi)
        c["p1"], c["m1"] = move(vps[0], u + 1, v), move(vps[1], u + 1, v)
        yield
        c["uc"].wait_recv()
        c["ud"].wait_recv()
        c["p2"], c["m2"] = move(vps[0], u + 2, v), move(vps[1], u + 2, v)
        yield
        c["m3"].wait_recv()
        c["f3"] = move(vps[1], u + 3, v + 1)
        yield
        c["p1"].wait_recv()
        c["f1"] = move(vps[0], u + 1, v + 3)
        yield
        c["m2"].wait_recv()
        c["f2"] = move(vps[1], u + 2, v + 1)
        yield
        for name in ("m0", "m1", "p3", "p2", "f0", "f3", "f1", "f2"):
            c[name].wait_recv()
        yield

    def col_sum(j):
        def blocks(xx, first=0, count=4):
            return part.at[j, pl.ds((xx % 4) * 4 + first, count)]

        def piece(hh, start=0, count=bp):
            return part.at[j, x * 4 + hh % 4, pl.ds(start, count)]

        c = {}

        def partial(xx):
            base = pl.multiple_of((xx % 4) * (4 * bp), 4 * bp)
            span = pl.ds(base, 4 * bp)
            units = pl.ds(j * LC, LC)
            value = product(
                (gp_hi[span], gp_lo[span]), (wout_hi[units], wout_lo[units]), NT
            )
            part[j, pl.ds((xx % 4) * 4, 4)] = value.reshape(4, bp, LC)

        partial(x + 2)
        c["a"] = send(blocks(x + 2, 0, 2), rx1.at[j, 0], xp)
        c["b"] = send(blocks(x + 2, 2, 2), rx1.at[j, 1], xm)
        yield
        partial(x + 1)
        c["c"] = send(blocks(x + 1, 2, 2), rx2.at[j, 0, pl.ds(2, 2)], xp)
        yield
        partial(x + 3)
        c["d"] = send(blocks(x + 3, 0, 2), rx2.at[j, 1, pl.ds(0, 2)], xm)
        yield
        partial(x)
        yield
        c["a"].wait_recv()
        part[j, pl.ds(((x + 1) % 4) * 4, 2)] += rx1[j, 0]
        c["e"] = send(blocks(x + 1, 0, 2), rx2.at[j, 0, pl.ds(0, 2)], xp)
        yield
        c["b"].wait_recv()
        part[j, pl.ds(((x + 3) % 4) * 4 + 2, 2)] += rx1[j, 1]
        c["f"] = send(blocks(x + 3, 2, 2), rx2.at[j, 1, pl.ds(2, 2)], xm)
        yield
        for name in ("c", "d", "e", "f"):
            c[name].wait_recv()
        part[j, pl.ds(x * 4, 4)] += rx2[j, 0] + rx2[j, 1]
        c["g"] = send(piece(zh + 2, 0, half), rz1.at[j, 0, pl.ds(0, half)], zp)
        c["h"] = send(piece(zh + 2, half, rest), rz1.at[j, 1, pl.ds(0, rest)], zm)
        c["i"] = send(piece(zh + 1, half, rest), rz2.at[j, 0, pl.ds(half, rest)], zp)
        c["k"] = send(piece(zh + 3, 0, half), rz2.at[j, 1, pl.ds(0, half)], zm)
        yield
        c["g"].wait_recv()
        part[j, x * 4 + (zh + 1) % 4, pl.ds(0, half)] += rz1[j, 0, pl.ds(0, half)]
        c["l"] = send(piece(zh + 1, 0, half), rz2.at[j, 0, pl.ds(0, half)], zp)
        yield
        c["h"].wait_recv()
        part[j, x * 4 + (zh + 3) % 4, pl.ds(half, rest)] += rz1[j, 1, pl.ds(0, rest)]
        c["m"] = send(piece(zh + 3, half, rest), rz2.at[j, 1, pl.ds(half, rest)], zm)
        yield
        for name in ("i", "k", "l", "m"):
            c[name].wait_recv()
        total = part[j, x * 4 + zh] + rz2[j, 0] + rz2[j, 1]
        mine = rows_buf[:, pl.ds(j * LC, LC)]
        slope = normal_cdf(mine) + mine * density(mine)
        pg[j, pl.ds(pl.multiple_of(col * bp, bp), bp)] = total * slope
        yield

    def pg_block(j):
        def block(xx, hh, start, count):
            first = pl.multiple_of((xx * 4 + hh) * bp + start, TILE)
            return pg.at[j, pl.ds(first, count)]

        return block

    def p_block(offset):
        def block(xx, hh, start, count):
            return p_all.at[pl.ds((xx * 4 + hh) * OWN + offset + start, count)]

        return block

    def quarters(body, parts):
        for k in range(parts):
            lax.fori_loop(k * steps // parts, (k + 1) * steps // parts, body, 0)
            yield

    def tables():
        live = [(kept_ref[s] + (TILE - 1)) // TILE for s in range(SAMPLES)]
        ends = []
        for s in range(SAMPLES):
            ends.append(live[s] + (ends[-1] if ends else 0))

        def fill(i, carry):
            source = i
            for s in range(SAMPLES):
                source = source + jnp.where(i >= ends[s], SAMPLE_TILES - live[s], 0)
            src[i] = jnp.where(i < ends[-1], source, -1)
            return carry

        lax.fori_loop(0, tb // TILE, fill, 0)
        for s in range(SAMPLES):
            begin = ends[s] - live[s]

            def place(i, carry, s=s, begin=begin):
                inv[s * SAMPLE_TILES + i] = jnp.where(i < live[s], begin + i, -1)
                return carry

            lax.fori_loop(0, SAMPLE_TILES, place, 0)
        yield

    def fetch(ref, first, count, masked):
        width = ref.shape[-1]

        def one(i, carry):
            at = src[first + i]
            tile = ref[jnp.maximum(at, 0)]
            if masked:
                tile = jnp.where(at >= 0, tile, 0.0)
            stage[pl.ds(pl.multiple_of(i * TILE, TILE), TILE), pl.ds(0, width)] = tile
            return carry

        lax.fori_loop(0, count, one, 0, unroll=4)
        return stage[pl.ds(0, count * TILE), pl.ds(0, width)]

    def pack_g():
        def body(t, carry):
            value = fetch(g_all, t * SAMPLE_TILES, SAMPLE_TILES, True)
            span = pl.ds(pl.multiple_of(t * PAD, PAD), PAD)
            gp_hi[span], gp_lo[span] = split(value)
            return carry

        yield from quarters(body, 1)

    def transposed(ref, to_hi, to_lo, masked):
        def body(t, carry):
            value = fetch(ref, t * SAMPLE_TILES, SAMPLE_TILES, masked).T
            high, low = split(value)
            to_hi[t] = high
            to_lo[t] = low
            return carry

        yield from quarters(body, 2)

    def own_rows():
        def one(i, carry):
            at = src[col * (bp // TILE) + i]
            rows_buf[pl.ds(pl.multiple_of(i * TILE, TILE), TILE)] = p_all[jnp.maximum(at, 0)]
            return carry

        lax.fori_loop(0, bp // TILE, one, 0)
        yield

    def w_out_split():
        weights[0].wait()
        wout_hi[...], wout_lo[...] = split(wout_f[...])
        yield

    def w_in_split():
        weights[1].wait()
        for j in range(J):
            win_hi[j], win_lo[j] = split(win_f[:, pl.ds(j * LC, LC)])
        yield

    def w_out_grad():
        dwt[...] = jnp.zeros_like(dwt)

        def body(t, carry):
            value = fetch(p_all, t * SAMPLE_TILES, SAMPLE_TILES, False)
            act = split(value * normal_cdf(value))
            dwt[...] += product((gt_hi[t], gt_lo[t]), act, NN)
            return carry

        yield from quarters(body, 4)
        dwout_ref[...] = dwt[...].T
        yield

    def w_in_grad(j):
        units = pl.ds(j * LC, LC)

        def body(t, carry):
            value = split(pg[j, pl.ds(pl.multiple_of(t * PAD, PAD), PAD)])
            dwin_ref[:, units] += product((xt_hi[t], xt_lo[t]), value, NN)
            return carry

        dwin_ref[:, units] = jnp.zeros((D, LC), F32)
        yield from quarters(body, 2)

    def x_grad(j):
        def body(t, carry):
            value = split(pg[j, pl.ds(pl.multiple_of(t * PAD, PAD), PAD)])
            out = product(value, (win_hi[j], win_lo[j]), NT).reshape(SAMPLE_TILES, TILE, D)
            span = pl.ds(t * SAMPLE_TILES, SAMPLE_TILES)
            if j == 0:
                dxp[span] = out
            else:
                dxp[span] += out
            return carry

        yield from quarters(body, 4)

    def row_sum():
        def spread(yy, cc):
            yy = yy % 4

            def one(i, carry):
                ll = i // OWN
                at = inv[(yy * 4 + ll * 2 + cc) * OWN + i % OWN]
                tile = dxp[jnp.maximum(at, 0)]
                dxs[cc, yy, i] = jnp.where(at >= 0, tile, 0.0)
                return carry

            lax.fori_loop(0, 2 * OWN, one, 0, unroll=4)

        order = (y + 2, y + 1, y + 3, y)
        s = []
        for k, yy in enumerate(order):
            spread(yy, 1 - core)
            s.append(send(dxs.at[1 - core, yy % 4], dsib.at[k], sib))
        yield
        for yy in order:
            spread(yy, core)

        def blocks(yy, ll):
            return dxs.at[core, yy % 4, pl.ds(ll * OWN, OWN)]

        def add_sib(k):
            s[k].wait_recv()
            dxs[core, order[k] % 4] += dsib[k]

        yield
        c = {}
        add_sib(0)
        c["a"] = send(blocks(y + 2, 0), dy1.at[0], yp)
        c["b"] = send(blocks(y + 2, 1), dy1.at[1], ym)
        yield
        add_sib(1)
        c["c"] = send(blocks(y + 1, 1), dy2.at[0, pl.ds(OWN, OWN)], yp)
        yield
        add_sib(2)
        c["d"] = send(blocks(y + 3, 0), dy2.at[1, pl.ds(0, OWN)], ym)
        yield
        add_sib(3)
        yield
        c["a"].wait_recv()
        dxs[core, (y + 1) % 4, pl.ds(0, OWN)] += dy1[0]
        c["e"] = send(blocks(y + 1, 0), dy2.at[0, pl.ds(0, OWN)], yp)
        yield
        c["b"].wait_recv()
        dxs[core, (y + 3) % 4, pl.ds(OWN, OWN)] += dy1[1]
        c["f"] = send(blocks(y + 3, 1), dy2.at[1, pl.ds(OWN, OWN)], ym)
        yield
        for name in ("c", "d", "e", "f"):
            c[name].wait_recv()
        dxs[core, y] += dy2[0] + dy2[1]
        c["z"] = send(blocks(y, 1 - zl), dz, zlp)
        yield
        c["z"].wait_recv()
        dx_ref[...] = dxs[core, y, pl.ds(zl * OWN, OWN)] + dz[...]
        yield

    parts = {
        "g": row_gather(g_all),
        "x": row_gather(x_all),
        "p": col_gather(p_block(0), OWN - CROSS),
        "q": col_gather(p_block(OWN - CROSS), CROSS, z_first=False),
        "tab": tables(),
        "wo": w_out_split(),
        "wi": w_in_split(),
        "pack": pack_g(),
        "own": own_rows(),
        "gt": transposed(g_all, gt_hi, gt_lo, True),
        "xt": transposed(x_all, xt_hi, xt_lo, False),
        "dwo": w_out_grad(),
        "t": row_sum(),
    }
    for j in range(J):
        parts[f"s{j}"] = col_sum(j)
        parts[f"a{j}"] = col_gather(pg_block(j), bp)
        parts[f"dx{j}"] = x_grad(j)
        parts[f"dw{j}"] = w_in_grad(j)
    for name in ORDER:
        next(parts[name])
    for part_left in parts.values():
        assert next(part_left, None) is None
    for copy in started:
        copy.wait_send()
    assert len(started) <= COPIES


def grad_kernel(tb, out_grad, inputs, pre_act, w_in, w_out, kept):
    bp = tb // 16
    vmem = pl.BlockSpec(memory_space=pltpu.VMEM)
    anywhere = pl.BlockSpec(memory_space=pl.ANY)

    def room(*shape, dtype=F32):
        return pltpu.VMEM(shape, dtype)

    half = functools.partial(room, dtype=BF16)
    steps = tb // PAD
    dx, dwin, dwout = pl.pallas_call(
        functools.partial(kernel, tb),
        out_shape=(
            jax.ShapeDtypeStruct((OWN, TILE, D), F32),
            jax.ShapeDtypeStruct((D, F), F32),
            jax.ShapeDtypeStruct((F, D), F32),
        ),
        in_specs=[pl.BlockSpec(memory_space=pltpu.SMEM), vmem, vmem, vmem, anywhere, anywhere],
        out_specs=(vmem, vmem, vmem),
        scratch_shapes=[
            pltpu.SMEM((tb // TILE,), jnp.int32),
            pltpu.SMEM((TILES,), jnp.int32),
            room(TILES, TILE, D),
            room(TILES, TILE, D),
            room(TILES, TILE, F),
            room(J, 16, bp, LC),
            room(J, 2, 2, bp, LC),
            room(J, 2, 4, bp, LC),
            room(J, 2, bp - bp // 16 * 8, LC),
            room(J, 2, bp, LC),
            room(J, tb, LC),
            half(tb, D),
            half(tb, D),
            half(steps, D, PAD),
            half(steps, D, PAD),
            half(steps, D, PAD),
            half(steps, D, PAD),
            room(D, F),
            room(F, D),
            half(J, D, LC),
            half(J, D, LC),
            half(F, D),
            half(F, D),
            room(tb // TILE, TILE, D),
            room(2, 4, 2 * OWN, TILE, D),
            room(4, 2 * OWN, TILE, D),
            room(2, OWN, TILE, D),
            room(2, 2 * OWN, TILE, D),
            room(OWN, TILE, D),
            room(D, F),
            room(PAD, F),
            room(bp, F),
            pltpu.SemaphoreType.DMA((COPIES,)),
            pltpu.SemaphoreType.DMA((COPIES,)),
            pltpu.SemaphoreType.DMA((2,)),
        ],
        compiler_params=pltpu.CompilerParams(
            collective_id=tb // PAD, has_side_effects=True, vmem_limit_bytes=64 * 1024 * 1024
        ),
        cost_estimate=pl.CostEstimate(flops=12 * tb * D * F * 2, bytes_accessed=6 * 1024 * 1024, transcendentals=0),
    )(
        kept,
        out_grad.reshape(OWN, TILE, D),
        inputs.reshape(OWN, TILE, D),
        pre_act.reshape(OWN, TILE, F),
        w_in,
        w_out,
    )
    return dx.reshape(ROWS, D), dwin, dwout


def shards(*args):
    tiles = jnp.sum((args[-1] + (TILE - 1)) // TILE)
    index = sum((tiles > rows // TILE).astype(jnp.int32) for rows in BUCKETS[:-1])
    return lax.switch(index, [functools.partial(grad_kernel, rows) for rows in BUCKETS], *args)


def solution(mesh):
    return jax.shard_map(
        shards,
        mesh=mesh,
        in_specs=(
            P("row", "col"),
            P("row", "col"),
            P("col", "row"),
            P("col", "row"),
            P("row", "col"),
            P(),
        ),
        out_specs=(P("row", "col"), P("col", "row"), P("row", "col")),
        check_vma=False,
    )
```

```python
import functools
import math

import jax
import jax.numpy as jnp
from jax import lax
from jax.experimental import pallas as pl
from jax.experimental.pallas import tpu as pltpu
from jax.sharding import PartitionSpec as P

PAD = 256
SAMPLES = 8
TOKENS = 2048
TILE = 8
SAMPLE_TILES = PAD // TILE
TILES = TOKENS // TILE
ROWS = 128
OWN = ROWS // TILE
D = 384
F = 768
COPIES = 192
HALVES = 16
ORDER = (
    "g", "o", "tab", "tab", "tab", "tab", "o", "wo", "q", "g", "g", "g", "o", "o", "p", "g", "g", "q", "q", "q",
    "g", "o", "o", "o", "p", "g", "q", "g", "pack", "o", "s0", "wi", "p", "p", "o", "own", "q", "s0", "s0", "s1",
    "gt", "gt", "q", "q", "s0", "s1", "s1", "s2", "p", "p", "p", "q", "s1", "s0", "s0", "s2", "s2", "s1", "s1",
    "s0", "a0", "p", "s1", "a1", "s2", "a0", "a0", "a0", "p", "a1", "a1", "a1", "x", "s2", "s2", "dwo", "a0",
    "a0", "dwo", "s2", "a0", "a2", "a1", "a1", "dwo", "a0", "a1", "dwf", "a1", "a2", "a2", "a2", "x", "x", "x",
    "a0", "dx0", "a2", "a1", "dx1", "a2", "t0", "t0", "a2", "x", "x", "t0", "x", "a2", "t0", "t0", "t0", "t0",
    "a2", "dx2", "t1", "t1", "t0", "x", "t1", "t1", "t1", "t1", "x", "xt", "t1", "t0", "t1", "xt", "dw0", "t0",
    "t1", "dw1", "dw2", "t1",
)
PLANS = {10: ((4, 4, 2), 5), 12: ((4, 4, 4), 6), 16: ((6, 6, 4), 8)}
LC = 256
LANES = F // LC
MESH = pl.DeviceIdType.MESH
F32 = jnp.float32
BF16 = jnp.bfloat16


def split(value):
    high = value.astype(BF16)
    return high, (value - high.astype(F32)).astype(BF16)


def product(left, right):
    def one(a, b):
        return jnp.dot(a, b, preferred_element_type=F32)

    (lh, ll), (rh, rl) = left, right
    return one(lh, rh) + (one(ll, rh) + one(lh, rl))


def normal_cdf(value):
    return 0.5 * (1.0 + lax.erf(value * (1.0 / math.sqrt(2.0))))


def density(value):
    return jnp.exp(-0.5 * value * value) * (1.0 / math.sqrt(2.0 * math.pi))


def cumulative(values):
    ends, total = [], 0
    for value in values:
        total = total + value
        ends.append(total)
    return ends


def kernel(
    slots, chunks, cross,
    kept_ref, g_ref, x_ref, p_ref, win_hbm, wout_hbm,
    dx_ref, dwin_ref, dwout_ref,
    src, inv,
    g_all, x_all, p_main, p_over, part, rx1, rx2, rz1, rz2, pg,
    gp_hi, gp_lo, gt_hi, gt_lo, xt_hi, xt_lo,
    win_f, wout_f, win_hi, win_lo, wout_hi, wout_lo,
    dxp, dxs, dsib, dy1, dy2, dz, dwt, acc, stage, mine, counts,
    send_sem, recv_sem, local_sem,
):
    spare = OWN - slots
    first_slot = [end - t for end, t in zip(cumulative(chunks), chunks)]
    row, col = lax.axis_index("row"), lax.axis_index("col")
    y, zl, core = row // 4, (row // 2) % 2, row % 2
    x, zh = col // 4, col % 4

    def at_row(yy, ll, cc):
        return {"row": (yy % 4) * 4 + ll * 2 + cc, "col": col}

    def at_col(xx, hh):
        return {"row": row, "col": (xx % 4) * 4 + hh % 4}

    xp, xm = at_col(x + 1, zh), at_col(x + 3, zh)
    zp, zm = at_col(x, zh + 1), at_col(x, zh + 3)
    yp, ym = at_row(y + 1, zl, core), at_row(y + 3, zl, core)
    zlp, sib = at_row(y, 1 - zl, core), at_row(y, zl, 1 - core)
    peers = (xp, xm, zp, zm, yp, ym, zlp, sib)

    barrier = pltpu.get_barrier_semaphore()
    for peer in peers:
        pl.semaphore_signal(barrier, inc=1, device_id=peer, device_id_type=MESH)

    weights = [
        pltpu.make_async_copy(wout_hbm, wout_f, local_sem.at[0]),
        pltpu.make_async_copy(win_hbm, win_f, local_sem.at[1]),
    ]
    for w in weights:
        w.start()

    started = []

    def send(source, target, peer):
        k = len(started)
        copy = pltpu.make_async_remote_copy(
            src_ref=source, dst_ref=target, send_sem=send_sem.at[k], recv_sem=recv_sem.at[k],
            device_id=peer, device_id_type=MESH,
        )
        copy.start()
        started.append(copy)
        return copy

    limit = kept_ref[row // 2] - (row % 2) * ROWS
    position = lax.broadcasted_iota(jnp.int32, (OWN, TILE, D), 0) * TILE + lax.broadcasted_iota(
        jnp.int32, (OWN, TILE, D), 1
    )
    g_all[pl.ds(row * OWN, OWN)] = jnp.where(position < limit, g_ref[...], 0.0)
    x_all[pl.ds(row * OWN, OWN)] = x_ref[...]
    p_main[pl.ds(col * slots, slots)] = p_ref[pl.ds(0, slots)]
    if spare:
        p_over[pl.ds(col * spare, spare)] = p_ref[pl.ds(slots, spare)]

    pl.semaphore_wait(barrier, len(peers))

    def lanes(n):
        return pl.ds(pl.multiple_of(n * LC, LC), LC)

    def row_gather(ref):
        def block(yy, ll, cc):
            return ref.at[pl.ds(((yy % 4) * 4 + ll * 2 + cc) * OWN, OWN)]

        def move(peer, *where):
            return send(block(*where), block(*where), peer)

        own = (y, zl, core)
        c = {"z": move(zlp, *own), "up": move(yp, *own), "down": move(ym, *own)}
        s = [move(sib, *own)]
        yield
        c["z"].wait_recv()
        other = (y, 1 - zl, core)
        c["up2"], c["down2"] = move(yp, *other), move(ym, *other)
        s.append(move(sib, *other))
        yield
        c["up"].wait_recv()
        c["far"] = move(yp, y + 3, zl, core)
        s.append(move(sib, y + 3, zl, core))
        yield
        c["down"].wait_recv()
        s.append(move(sib, y + 1, zl, core))
        yield
        c["down2"].wait_recv()
        c["far2"] = move(ym, y + 1, 1 - zl, core)
        s.append(move(sib, y + 1, 1 - zl, core))
        yield
        c["up2"].wait_recv()
        s.append(move(sib, y + 3, 1 - zl, core))
        yield
        c["far"].wait_recv()
        s.append(move(sib, y + 2, zl, core))
        yield
        c["far2"].wait_recv()
        s.append(move(sib, y + 2, 1 - zl, core))
        yield
        for copy in s:
            copy.wait_recv()
        yield

    def col_gather(block, size, z_first=True):
        cut = size // 2 if size < 16 else size // 16 * TILE
        lo, hi = (0, cut), (cut, size - cut)
        u, v, ups, vps = (zh, x, (zp, zm), (xp, xm)) if z_first else (x, zh, (xp, xm), (zp, zm))

        def move(peer, uu, vv, span=(0, size)):
            xx, hh = (vv, uu) if z_first else (uu, vv)
            ref = block(xx % 4, hh % 4, *span)
            return send(ref, ref, peer)

        c = {}
        c["ua"], c["ub"] = move(ups[0], u, v), move(ups[1], u, v)
        c["p0"], c["m0"] = move(vps[0], u, v), move(vps[1], u, v)
        yield
        c["p0"].wait_recv()
        c["f0"] = move(vps[0], u, v + 3)
        yield
        c["ua"].wait_recv()
        c["uc"] = move(ups[0], u + 3, v, lo)
        c["p3"], c["m3"] = move(vps[0], u + 3, v), move(vps[1], u + 3, v)
        yield
        c["ub"].wait_recv()
        c["ud"] = move(ups[1], u + 1, v, hi)
        c["p1"], c["m1"] = move(vps[0], u + 1, v), move(vps[1], u + 1, v)
        yield
        c["uc"].wait_recv()
        c["ud"].wait_recv()
        c["p2"], c["m2"] = move(vps[0], u + 2, v), move(vps[1], u + 2, v)
        yield
        c["m3"].wait_recv()
        c["f3"] = move(vps[1], u + 3, v + 1)
        yield
        c["p1"].wait_recv()
        c["f1"] = move(vps[0], u + 1, v + 3)
        yield
        c["m2"].wait_recv()
        c["f2"] = move(vps[1], u + 2, v + 1)
        yield
        for name in ("m0", "m1", "p3", "p2", "f0", "f3", "f1", "f2"):
            c[name].wait_recv()
        yield

    def col_sum(j):
        bp = chunks[j] * TILE
        half = bp // 16 * TILE
        rest = bp - half

        def blocks(xx, first=0, count=4):
            return part[j].at[pl.ds((xx % 4) * 4 + first, count)]

        def piece(hh, start, count):
            return part[j].at[x * 4 + hh % 4, pl.ds(start, count)]

        c = {}

        span = pl.ds(HALVES * TILE * first_slot[j], HALVES * bp)
        left = gp_hi[span], gp_lo[span]

        def body(n, carry):
            value = product(left, (wout_hi[n], wout_lo[n])).reshape(HALVES, bp, LC)
            part[j][:, :, lanes(n)] = value
            return carry

        lax.fori_loop(0, LANES, body, 0)
        c["a"] = send(blocks(x + 2, 0, 2), rx1[j].at[0], xp)
        c["b"] = send(blocks(x + 2, 2, 2), rx1[j].at[1], xm)
        c["c"] = send(blocks(x + 1, 2, 2), rx2[j].at[0, pl.ds(2, 2)], xp)
        c["d"] = send(blocks(x + 3, 0, 2), rx2[j].at[1, pl.ds(0, 2)], xm)
        yield
        c["a"].wait_recv()
        part[j][pl.ds(((x + 1) % 4) * 4, 2)] += rx1[j][0]
        c["e"] = send(blocks(x + 1, 0, 2), rx2[j].at[0, pl.ds(0, 2)], xp)
        yield
        c["b"].wait_recv()
        part[j][pl.ds(((x + 3) % 4) * 4 + 2, 2)] += rx1[j][1]
        c["f"] = send(blocks(x + 3, 2, 2), rx2[j].at[1, pl.ds(2, 2)], xm)
        yield
        for name in ("c", "d", "e", "f"):
            c[name].wait_recv()
        part[j][pl.ds(x * 4, 4)] += rx2[j][0] + rx2[j][1]
        c["g"] = send(piece(zh + 2, 0, half), rz1[j].at[0, pl.ds(0, half)], zp)
        c["h"] = send(piece(zh + 2, half, rest), rz1[j].at[1, pl.ds(0, rest)], zm)
        c["i"] = send(piece(zh + 1, half, rest), rz2[j].at[0, pl.ds(half, rest)], zp)
        c["k"] = send(piece(zh + 3, 0, half), rz2[j].at[1, pl.ds(0, half)], zm)
        yield
        c["g"].wait_recv()
        part[j][x * 4 + (zh + 1) % 4, pl.ds(0, half)] += rz1[j][0, pl.ds(0, half)]
        c["l"] = send(piece(zh + 1, 0, half), rz2[j].at[0, pl.ds(0, half)], zp)
        yield
        c["h"].wait_recv()
        part[j][x * 4 + (zh + 3) % 4, pl.ds(half, rest)] += rz1[j][1, pl.ds(0, rest)]
        c["m"] = send(piece(zh + 3, half, rest), rz2[j].at[1, pl.ds(half, rest)], zm)
        yield
        for name in ("i", "k", "l", "m"):
            c[name].wait_recv()
        total = part[j][x * 4 + zh] + rz2[j][0] + rz2[j][1]
        rows = mine[j][...]
        slope = normal_cdf(rows) + rows * density(rows)
        pg[j][pl.ds(pl.multiple_of(col * bp, bp), bp)] = total * slope
        yield

    def pg_block(j):
        bp = chunks[j] * TILE

        def block(xx, hh, start, count):
            first = pl.multiple_of((xx * 4 + hh) * bp + start, TILE)
            return pg[j].at[pl.ds(first, count)]

        return block

    def p_block(ref, per_block, offset):
        def block(xx, hh, start, count):
            return ref.at[pl.ds((xx * 4 + hh) * per_block + offset + start, count)]

        return block

    def tables():
        live = [
            jnp.clip((kept_ref[b // 2] + (TILE - 1)) // TILE - b % 2 * OWN, 0, OWN)
            for b in range(HALVES)
        ]
        kept_here = [jnp.minimum(n, slots) for n in live]
        over = [n - k for n, k in zip(live, kept_here)]
        over_end = cumulative(over)
        free_end = cumulative([slots - k for k in kept_here])
        for b in range(HALVES):
            counts[0, b] = live[b]
            counts[1, b] = kept_here[b]
            counts[2, b] = over_end[b] - over[b]
            counts[3, b] = free_end[b] - slots
        yield

        def fill_block(b, carry):
            here, free = counts[1, b], counts[3, b]
            for j, t in enumerate(chunks):

                def fill(i, carry, j=j, t=t):
                    k = first_slot[j] + i
                    at = -1
                    if spare:
                        e = free + k
                        moved = e + slots
                        for n in range(HALVES - 1):
                            moved = moved + jnp.where(e >= over_end[n], OWN - over[n], 0)
                        at = jnp.where(e < over_end[-1], moved, -1)
                    src[HALVES * first_slot[j] + b * t + i] = jnp.where(k < here, b * OWN + k, at)
                    return carry

                lax.fori_loop(0, t, fill, 0)
            return carry

        lax.fori_loop(0, HALVES // 2, fill_block, 0)
        yield
        lax.fori_loop(HALVES // 2, HALVES, fill_block, 0)
        yield

        def place_block(b, carry):
            here = counts[0, b]

            def stay(k, carry):
                inv[b * OWN + k] = jnp.where(k < here, b * slots + k, -1)
                return carry

            lax.fori_loop(0, slots, stay, 0)
            if spare:
                begin = counts[2, b]

                def leave(i, carry):
                    e = begin + i
                    slot = e + kept_here[0]
                    for n in range(HALVES - 1):
                        slot = slot + jnp.where(e >= free_end[n], kept_here[n + 1], 0)
                    inv[b * OWN + slots + i] = jnp.where(slots + i < here, slot, -1)
                    return carry

                lax.fori_loop(0, spare, leave, 0)
            return carry

        lax.fori_loop(0, HALVES, place_block, 0)
        yield

    strips = slots // 2

    def fetch(ref, strip, masked):
        width = ref.shape[-1]

        def one(i, carry):
            at = src[strip * SAMPLE_TILES + i]
            tile = ref[jnp.maximum(at, 0)]
            if masked:
                tile = jnp.where(at >= 0, tile, 0.0)
            stage[pl.ds(pl.multiple_of(i * TILE, TILE), TILE), pl.ds(0, width)] = tile
            return carry

        lax.fori_loop(0, SAMPLE_TILES, one, 0, unroll=4)
        return stage[:, pl.ds(0, width)]

    def moved_tile(at, tile):
        if not spare:
            return tile
        at = jnp.maximum(at, 0)
        place = at % OWN - slots
        index = at // OWN * spare + jnp.maximum(place, 0)
        return jnp.where(place >= 0, p_over[index], tile)

    def fetch_p(strip, j):
        def one(i, carry):
            n = (strip - first_slot[j] // 2) * SAMPLE_TILES + i
            own = p_main[n // chunks[j] * slots + first_slot[j] + n % chunks[j]]
            at = src[strip * SAMPLE_TILES + i]
            stage[pl.ds(pl.multiple_of(i * TILE, TILE), TILE)] = moved_tile(at, own)
            return carry

        lax.fori_loop(0, SAMPLE_TILES, one, 0, unroll=4)

    def own_rows():
        for j, t in enumerate(chunks):

            def one(i, carry, j=j, t=t):
                at = src[HALVES * first_slot[j] + col * t + i]
                mine[j][pl.ds(pl.multiple_of(i * TILE, TILE), TILE)] = moved_tile(
                    at, p_ref[first_slot[j] + i]
                )
                return carry

            lax.fori_loop(0, t, one, 0)
        yield

    def pack_g():
        def body(strip, carry):
            span = pl.ds(pl.multiple_of(strip * PAD, PAD), PAD)
            gp_hi[span], gp_lo[span] = split(fetch(g_all, strip, True))
            return carry

        lax.fori_loop(0, strips, body, 0)
        yield

    def transposed(ref, to_hi, to_lo, masked):
        def body(strip, carry):
            high, low = split(fetch(ref, strip, masked).T)
            to_hi[strip] = high
            to_lo[strip] = low
            return carry

        lax.fori_loop(0, strips // 2, body, 0)
        yield
        lax.fori_loop(strips // 2, strips, body, 0)
        yield

    def w_out_split():
        weights[0].wait()

        def body(n, carry):
            rows = pl.ds(pl.multiple_of(n * LC, LC), LC)
            wout_hi[n], wout_lo[n] = split(wout_f[rows].T)
            return carry

        lax.fori_loop(0, LANES, body, 0)
        yield

    def w_in_split():
        weights[1].wait()

        def body(n, carry):
            win_hi[n], win_lo[n] = split(win_f[:, lanes(n)].T)
            return carry

        lax.fori_loop(0, LANES, body, 0)
        yield

    def w_out_grad():
        dwt[...] = jnp.zeros_like(dwt)
        for j, t in enumerate(chunks):

            def body(strip, carry, j=j):
                fetch_p(strip, j)
                left = gt_hi[strip], gt_lo[strip]

                def step(n, carry):
                    value = stage[:, lanes(n)]
                    dwt[n] += product(left, split(value * normal_cdf(value)))
                    return carry

                return lax.fori_loop(0, LANES, step, carry)

            lax.fori_loop(first_slot[j] // 2, (first_slot[j] + t) // 2, body, 0)
            yield

    def w_out_last():
        def body(n, carry):
            dwout_ref[pl.ds(pl.multiple_of(n * LC, LC), LC)] = dwt[n].T
            return carry

        lax.fori_loop(0, LANES, body, 0)
        yield

    def w_in_grad(j):
        if j == 0:
            dwin_ref[...] = jnp.zeros_like(dwin_ref)

        def body(i, carry):
            strip = first_slot[j] // 2 + i
            span = pl.ds(pl.multiple_of(i * PAD, PAD), PAD)
            left = xt_hi[strip], xt_lo[strip]

            def step(n, carry):
                dwin_ref[:, lanes(n)] += product(left, split(pg[j][span, lanes(n)]))
                return carry

            return lax.fori_loop(0, LANES, step, carry)

        lax.fori_loop(0, chunks[j] // 2, body, 0)
        yield

    def x_grad(j):
        t = chunks[j]

        def body(i, carry):
            span = pl.ds(pl.multiple_of(i * PAD, PAD), PAD)
            acc[...] = jnp.zeros_like(acc)

            def step(n, carry):
                left = split(pg[j][span, lanes(n)])
                acc[...] += product(left, (win_hi[n], win_lo[n])).reshape(acc.shape)
                return carry

            lax.fori_loop(0, LANES, step, carry)

            def place(q, carry):
                tile = i * SAMPLE_TILES + q
                dxp[tile // t * slots + first_slot[j] + tile % t] = acc[q]
                return carry

            return lax.fori_loop(0, SAMPLE_TILES, place, carry, unroll=4)

        lax.fori_loop(0, t // 2, body, 0)
        yield

    def row_sum(n, low, high):
        size = high - low

        def spread(yy, cc):
            yy = yy % 4

            def one(i, carry):
                ll, k = i // size, i % size
                at = inv[(yy * 4 + ll * 2 + cc) * OWN + low + k]
                tile = dxp[jnp.maximum(at, 0)]
                dxs[n][cc, yy, i] = jnp.where(at >= 0, tile, 0.0)
                return carry

            lax.fori_loop(0, 2 * size, one, 0, unroll=2)

        order = (y + 2, y + 1, y + 3, y)
        s = []
        for k, yy in enumerate(order):
            spread(yy, 1 - core)
            s.append(send(dxs[n].at[1 - core, yy % 4], dsib[n].at[k], sib))
        yield
        for yy in order:
            spread(yy, core)

        def blocks(yy, ll):
            return dxs[n].at[core, yy % 4, pl.ds(ll * size, size)]

        def add_sib(k):
            s[k].wait_recv()
            dxs[n][core, order[k] % 4] += dsib[n][k]

        yield
        c = {}
        add_sib(0)
        c["a"] = send(blocks(y + 2, 0), dy1[n].at[0], yp)
        c["b"] = send(blocks(y + 2, 1), dy1[n].at[1], ym)
        yield
        add_sib(1)
        c["c"] = send(blocks(y + 1, 1), dy2[n].at[0, pl.ds(size, size)], yp)
        yield
        add_sib(2)
        c["d"] = send(blocks(y + 3, 0), dy2[n].at[1, pl.ds(0, size)], ym)
        yield
        add_sib(3)
        yield
        c["a"].wait_recv()
        dxs[n][core, (y + 1) % 4, pl.ds(0, size)] += dy1[n][0]
        c["e"] = send(blocks(y + 1, 0), dy2[n].at[0, pl.ds(0, size)], yp)
        yield
        c["b"].wait_recv()
        dxs[n][core, (y + 3) % 4, pl.ds(size, size)] += dy1[n][1]
        c["f"] = send(blocks(y + 3, 1), dy2[n].at[1, pl.ds(size, size)], ym)
        yield
        for name in ("c", "d", "e", "f"):
            c[name].wait_recv()
        dxs[n][core, y] += dy2[n][0] + dy2[n][1]
        c["z"] = send(blocks(y, 1 - zl), dz[n], zlp)
        yield
        c["z"].wait_recv()
        dx_ref[pl.ds(low, size)] = dxs[n][core, y, pl.ds(zl * size, size)] + dz[n][...]
        yield

    early = first_slot[-1]
    parts = {
        "g": row_gather(g_all),
        "x": row_gather(x_all),
        "p": col_gather(p_block(p_main, slots, cross), slots - cross),
        "q": col_gather(p_block(p_main, slots, 0), cross, z_first=False),
        "tab": tables(),
        "wo": w_out_split(),
        "wi": w_in_split(),
        "pack": pack_g(),
        "own": own_rows(),
        "gt": transposed(g_all, gt_hi, gt_lo, True),
        "xt": transposed(x_all, xt_hi, xt_lo, False),
        "dwo": w_out_grad(),
        "dwf": w_out_last(),
        "t0": row_sum(0, 0, early),
        "t1": row_sum(1, early, OWN),
    }
    if spare:
        parts["o"] = col_gather(p_block(p_over, spare, 0), spare)
    for j in range(len(chunks)):
        parts[f"s{j}"] = col_sum(j)
        parts[f"a{j}"] = col_gather(pg_block(j), chunks[j] * TILE)
        parts[f"dx{j}"] = x_grad(j)
        parts[f"dw{j}"] = w_in_grad(j)
    for name in ORDER:
        if name in parts:
            next(parts[name])
    for left in parts.values():
        assert next(left, None) is None
    for copy in started:
        copy.wait_send()
    assert len(started) <= COPIES


def grad_kernel(slots, out_grad, inputs, pre_act, w_in, w_out, kept):
    chunks, cross = PLANS[slots]
    spare = OWN - slots
    early = slots - chunks[-1]
    vmem = pl.BlockSpec(memory_space=pltpu.VMEM)
    anywhere = pl.BlockSpec(memory_space=pl.ANY)

    def room(*shape, dtype=F32):
        return pltpu.VMEM(shape, dtype)

    half = functools.partial(room, dtype=BF16)

    def each(make):
        return [make(t * TILE) for t in chunks]

    def both(make):
        return [make(early), make(OWN - early)]

    dx, dwin, dwout = pl.pallas_call(
        functools.partial(kernel, slots, chunks, cross),
        out_shape=(
            jax.ShapeDtypeStruct((OWN, TILE, D), F32),
            jax.ShapeDtypeStruct((D, F), F32),
            jax.ShapeDtypeStruct((F, D), F32),
        ),
        in_specs=[pl.BlockSpec(memory_space=pltpu.SMEM), vmem, vmem, vmem, anywhere, anywhere],
        out_specs=(vmem, vmem, vmem),
        scratch_shapes=[
            pltpu.SMEM((HALVES * slots,), jnp.int32),
            pltpu.SMEM((TILES,), jnp.int32),
            room(TILES, TILE, D),
            room(TILES, TILE, D),
            room(HALVES * slots, TILE, F),
            room(max(HALVES * spare, 1), TILE, F),
            each(lambda r: room(HALVES, r, F)),
            each(lambda r: room(2, 2, r, F)),
            each(lambda r: room(2, 4, r, F)),
            each(lambda r: room(2, r - r // 16 * TILE, F)),
            each(lambda r: room(2, r, F)),
            each(lambda r: room(HALVES * r, F)),
            half(HALVES * slots * TILE, D),
            half(HALVES * slots * TILE, D),
            half(slots // 2, D, PAD),
            half(slots // 2, D, PAD),
            half(slots // 2, D, PAD),
            half(slots // 2, D, PAD),
            room(D, F),
            room(F, D),
            half(LANES, LC, D),
            half(LANES, LC, D),
            half(LANES, D, LC),
            half(LANES, D, LC),
            room(HALVES * slots, TILE, D),
            both(lambda e: room(2, 4, 2 * e, TILE, D)),
            both(lambda e: room(4, 2 * e, TILE, D)),
            both(lambda e: room(2, e, TILE, D)),
            both(lambda e: room(2, 2 * e, TILE, D)),
            both(lambda e: room(e, TILE, D)),
            room(LANES, D, LC),
            room(SAMPLE_TILES, TILE, D),
            room(PAD, F),
            each(lambda r: room(r, F)),
            pltpu.SMEM((4, HALVES), jnp.int32),
            pltpu.SemaphoreType.DMA((COPIES,)),
            pltpu.SemaphoreType.DMA((COPIES,)),
            pltpu.SemaphoreType.DMA((2,)),
        ],
        compiler_params=pltpu.CompilerParams(
            collective_id=slots, has_side_effects=True, vmem_limit_bytes=64 * 1024 * 1024
        ),
        cost_estimate=pl.CostEstimate(flops=24 * slots * ROWS * D * F, bytes_accessed=6 * 1024 * 1024, transcendentals=0),
    )(
        kept,
        out_grad.reshape(OWN, TILE, D),
        inputs.reshape(OWN, TILE, D),
        pre_act.reshape(OWN, TILE, F),
        w_in,
        w_out,
    )
    return dx.reshape(ROWS, D), dwin, dwout


def settle_kernel(*refs):
    sources, targets, rooms, sems = refs[:3], refs[3:6], refs[6:9], refs[9]
    pieces = []
    for source, target, space in zip(sources, targets, rooms):
        rows = source.shape[0] // 2
        pieces += [
            tuple(ref.at[pl.ds(k * rows, rows)] for ref in (source, space, target)) for k in range(2)
        ]
    inward = [
        pltpu.make_async_copy(a, b, sems.at[0, k]) for k, (a, b, _) in enumerate(pieces)
    ]
    outward = [
        pltpu.make_async_copy(b, c, sems.at[1, k]) for k, (_, b, c) in enumerate(pieces)
    ]
    for copy in inward:
        copy.start()
    for first, second in zip(inward, outward):
        first.wait()
        second.start()
    for copy in outward:
        copy.wait()


def settle(*arrays):
    anywhere = pl.BlockSpec(memory_space=pl.ANY)
    return pl.pallas_call(
        settle_kernel,
        out_shape=tuple(jax.ShapeDtypeStruct(a.shape, a.dtype) for a in arrays),
        in_specs=[anywhere] * 3,
        out_specs=(anywhere,) * 3,
        scratch_shapes=[pltpu.VMEM(a.shape, a.dtype) for a in arrays]
        + [pltpu.SemaphoreType.DMA((2, 6))],
        compiler_params=pltpu.CompilerParams(vmem_limit_bytes=60 * 1024 * 1024),
    )(*arrays)


def shards(*args):
    tiles = jnp.sum((args[-1] + (TILE - 1)) // TILE)
    choices = sorted(PLANS)
    index = sum((tiles > HALVES * slots).astype(jnp.int32) for slots in choices[:-1])
    grads = lax.switch(index, [functools.partial(grad_kernel, slots) for slots in choices], *args)
    return settle(*grads)


def solution(mesh):
    return jax.shard_map(
        shards,
        mesh=mesh,
        in_specs=(
            P("row", "col"),
            P("row", "col"),
            P("col", "row"),
            P("col", "row"),
            P("row", "col"),
            P(),
        ),
        out_specs=(P("row", "col"), P("col", "row"), P("row", "col")),
        check_vma=False,
    )
```

```python
import functools
import math

import jax
import jax.numpy as jnp
from jax import lax
from jax.experimental import pallas as pl
from jax.experimental.pallas import tpu as pltpu
from jax.sharding import PartitionSpec as P

PAD = 256
SAMPLES = 8
TOKENS = 2048
TILE = 8
SAMPLE_TILES = PAD // TILE
TILES = TOKENS // TILE
ROWS = 128
OWN = ROWS // TILE
D = 384
F = 768
COPIES = 192
HALVES = 16
ORDER = (
    "g", "o", "tab", "tab", "tab", "tab", "o", "wo", "q", "g", "g", "g", "o", "o", "p", "g", "g", "q", "q", "q",
    "g", "o", "o", "o", "p", "g", "q", "g", "pack", "o", "s0", "wi", "p", "p", "o", "own", "q", "s0", "s0", "s1",
    "gt", "gt", "q", "q", "s0", "s1", "s1", "s2", "p", "p", "p", "q", "s1", "s0", "s0", "s2", "s2", "s1", "s1",
    "s0", "a0", "p", "s1", "a1", "s2", "a0", "a0", "a0", "p", "a1", "a1", "a1", "x", "s2", "s2", "dwo", "a0",
    "a0", "dwo", "s2", "a0", "a2", "a1", "a1", "dwo", "a0", "a1", "dwf", "a1", "a2", "a2", "a2", "x", "x", "x",
    "a0", "dx0", "a2", "a1", "dx1", "a2", "t0", "t0", "a2", "x", "x", "t0", "x", "a2", "t0", "t0", "t0", "t0",
    "a2", "dx2", "t1", "t1", "t0", "x", "t1", "t1", "t1", "t1", "x", "xt", "t1", "t0", "t1", "xt", "dw0", "t0",
    "t1", "dw1", "dw2", "t1",
)
ORDER_FULL = (
    "p", "g", "tab", "tab", "tab", "tab", "wo", "own", "q", "p", "g", "g", "g", "p", "p", "g", "g", "g", "g",
    "q", "q", "q", "g", "pack", "s0", "p", "p", "p", "wi", "gt", "q", "gt", "q", "s0", "s0", "s1", "x", "p", "q",
    "q", "s0", "s1", "s1", "s2", "q", "s0", "s0", "p", "dwo", "s0", "a0", "s1", "s2", "dwo", "s2", "dwo", "a0",
    "a0", "a0", "dwf", "s1", "s1", "s2", "a0", "a0", "x", "x", "x", "a0", "s1", "a1", "s2", "s2", "a0", "x", "x",
    "x", "a1", "x", "a1", "a1", "x", "xt", "a0", "s2", "a2", "dx0", "a1", "a1", "xt", "a1", "dw0", "a1", "a2",
    "a2", "a2", "a2", "a1", "dx1", "t0", "t0", "a2", "a2", "dw1", "t0", "t0", "t0", "a2", "t0", "a2", "dx2",
    "t0", "t0", "t1", "t1", "dw2", "t1", "t1", "t1", "t1", "t0", "t1", "t1", "t1", "t0", "t1",
)
PLANS = {10: ((4, 4, 2), 5), 12: ((4, 4, 4), 6), 16: ((6, 6, 4), 8)}
LC = 256
LANES = F // LC
MESH = pl.DeviceIdType.MESH
F32 = jnp.float32
BF16 = jnp.bfloat16


def split(value):
    high = value.astype(BF16)
    return high, (value - high.astype(F32)).astype(BF16)


def product(left, right):
    def one(a, b):
        return jnp.dot(a, b, preferred_element_type=F32)

    (lh, ll), (rh, rl) = left, right
    return one(lh, rh) + (one(ll, rh) + one(lh, rl))


def normal_cdf(value):
    return 0.5 * (1.0 + lax.erf(value * (1.0 / math.sqrt(2.0))))


def density(value):
    return jnp.exp(-0.5 * value * value) * (1.0 / math.sqrt(2.0 * math.pi))


def cumulative(values):
    ends, total = [], 0
    for value in values:
        total = total + value
        ends.append(total)
    return ends


def kernel(
    slots, chunks, cross,
    kept_ref, g_ref, x_ref, p_ref, win_hbm, wout_hbm,
    dx_ref, dwin_ref, dwout_ref,
    src, inv,
    g_all, x_all, p_main, p_over, part, rx1, rx2, rz1, rz2, pg,
    gp_hi, gp_lo, gt_hi, gt_lo, xt_hi, xt_lo,
    win_f, wout_f, win_hi, win_lo, wout_hi, wout_lo,
    dxp, dxs, dsib, dy1, dy2, dz, dwt, acc, stage, mine, counts,
    send_sem, recv_sem, local_sem,
):
    spare = OWN - slots
    first_slot = [end - t for end, t in zip(cumulative(chunks), chunks)]
    row, col = lax.axis_index("row"), lax.axis_index("col")
    y, zl, core = row // 4, (row // 2) % 2, row % 2
    x, zh = col // 4, col % 4

    def at_row(yy, ll, cc):
        return {"row": (yy % 4) * 4 + ll * 2 + cc, "col": col}

    def at_col(xx, hh):
        return {"row": row, "col": (xx % 4) * 4 + hh % 4}

    xp, xm = at_col(x + 1, zh), at_col(x + 3, zh)
    zp, zm = at_col(x, zh + 1), at_col(x, zh + 3)
    yp, ym = at_row(y + 1, zl, core), at_row(y + 3, zl, core)
    zlp, sib = at_row(y, 1 - zl, core), at_row(y, zl, 1 - core)
    peers = (xp, xm, zp, zm, yp, ym, zlp, sib)

    barrier = pltpu.get_barrier_semaphore()
    for peer in peers:
        pl.semaphore_signal(barrier, inc=1, device_id=peer, device_id_type=MESH)

    weights = [
        pltpu.make_async_copy(wout_hbm, wout_f, local_sem.at[0]),
        pltpu.make_async_copy(win_hbm, win_f, local_sem.at[1]),
    ]
    for w in weights:
        w.start()

    started = []

    def send(source, target, peer):
        k = len(started)
        copy = pltpu.make_async_remote_copy(
            src_ref=source, dst_ref=target, send_sem=send_sem.at[k], recv_sem=recv_sem.at[k],
            device_id=peer, device_id_type=MESH,
        )
        copy.start()
        started.append(copy)
        return copy

    limit = kept_ref[row // 2] - (row % 2) * ROWS
    position = lax.broadcasted_iota(jnp.int32, (OWN, TILE, D), 0) * TILE + lax.broadcasted_iota(
        jnp.int32, (OWN, TILE, D), 1
    )
    g_all[pl.ds(row * OWN, OWN)] = jnp.where(position < limit, g_ref[...], 0.0)
    x_all[pl.ds(row * OWN, OWN)] = x_ref[...]
    p_main[pl.ds(col * slots, slots)] = p_ref[pl.ds(0, slots)]
    if spare:
        p_over[pl.ds(col * spare, spare)] = p_ref[pl.ds(slots, spare)]

    pl.semaphore_wait(barrier, len(peers))

    def lanes(n):
        return pl.ds(pl.multiple_of(n * LC, LC), LC)

    def row_gather(ref):
        def block(yy, ll, cc):
            return ref.at[pl.ds(((yy % 4) * 4 + ll * 2 + cc) * OWN, OWN)]

        def move(peer, *where):
            return send(block(*where), block(*where), peer)

        own = (y, zl, core)
        c = {"z": move(zlp, *own), "up": move(yp, *own), "down": move(ym, *own)}
        s = [move(sib, *own)]
        yield
        c["z"].wait_recv()
        other = (y, 1 - zl, core)
        c["up2"], c["down2"] = move(yp, *other), move(ym, *other)
        s.append(move(sib, *other))
        yield
        c["up"].wait_recv()
        c["far"] = move(yp, y + 3, zl, core)
        s.append(move(sib, y + 3, zl, core))
        yield
        c["down"].wait_recv()
        s.append(move(sib, y + 1, zl, core))
        yield
        c["down2"].wait_recv()
        c["far2"] = move(ym, y + 1, 1 - zl, core)
        s.append(move(sib, y + 1, 1 - zl, core))
        yield
        c["up2"].wait_recv()
        s.append(move(sib, y + 3, 1 - zl, core))
        yield
        c["far"].wait_recv()
        s.append(move(sib, y + 2, zl, core))
        yield
        c["far2"].wait_recv()
        s.append(move(sib, y + 2, 1 - zl, core))
        yield
        for copy in s:
            copy.wait_recv()
        yield

    def col_gather(block, size, z_first=True):
        cut = size // 2 if size < 16 else size // 16 * TILE
        lo, hi = (0, cut), (cut, size - cut)
        u, v, ups, vps = (zh, x, (zp, zm), (xp, xm)) if z_first else (x, zh, (xp, xm), (zp, zm))

        def move(peer, uu, vv, span=(0, size)):
            xx, hh = (vv, uu) if z_first else (uu, vv)
            ref = block(xx % 4, hh % 4, *span)
            return send(ref, ref, peer)

        c = {}
        c["ua"], c["ub"] = move(ups[0], u, v), move(ups[1], u, v)
        c["p0"], c["m0"] = move(vps[0], u, v), move(vps[1], u, v)
        yield
        c["p0"].wait_recv()
        c["f0"] = move(vps[0], u, v + 3)
        yield
        c["ua"].wait_recv()
        c["uc"] = move(ups[0], u + 3, v, lo)
        c["p3"], c["m3"] = move(vps[0], u + 3, v), move(vps[1], u + 3, v)
        yield
        c["ub"].wait_recv()
        c["ud"] = move(ups[1], u + 1, v, hi)
        c["p1"], c["m1"] = move(vps[0], u + 1, v), move(vps[1], u + 1, v)
        yield
        c["uc"].wait_recv()
        c["ud"].wait_recv()
        c["p2"], c["m2"] = move(vps[0], u + 2, v), move(vps[1], u + 2, v)
        yield
        c["m3"].wait_recv()
        c["f3"] = move(vps[1], u + 3, v + 1)
        yield
        c["p1"].wait_recv()
        c["f1"] = move(vps[0], u + 1, v + 3)
        yield
        c["m2"].wait_recv()
        c["f2"] = move(vps[1], u + 2, v + 1)
        yield
        for name in ("m0", "m1", "p3", "p2", "f0", "f3", "f1", "f2"):
            c[name].wait_recv()
        yield

    def col_sum(j):
        bp = chunks[j] * TILE
        half = bp // 16 * TILE
        rest = bp - half

        def blocks(xx, first=0, count=4):
            return part[j].at[pl.ds((xx % 4) * 4 + first, count)]

        def piece(hh, start, count):
            return part[j].at[x * 4 + hh % 4, pl.ds(start, count)]

        c = {}

        span = pl.ds(HALVES * TILE * first_slot[j], HALVES * bp)
        left = gp_hi[span], gp_lo[span]

        def body(n, carry):
            value = product(left, (wout_hi[n], wout_lo[n])).reshape(HALVES, bp, LC)
            part[j][:, :, lanes(n)] = value
            return carry

        lax.fori_loop(0, LANES, body, 0)
        c["a"] = send(blocks(x + 2, 0, 2), rx1[j].at[0], xp)
        c["b"] = send(blocks(x + 2, 2, 2), rx1[j].at[1], xm)
        c["c"] = send(blocks(x + 1, 2, 2), rx2[j].at[0, pl.ds(2, 2)], xp)
        c["d"] = send(blocks(x + 3, 0, 2), rx2[j].at[1, pl.ds(0, 2)], xm)
        yield
        c["a"].wait_recv()
        part[j][pl.ds(((x + 1) % 4) * 4, 2)] += rx1[j][0]
        c["e"] = send(blocks(x + 1, 0, 2), rx2[j].at[0, pl.ds(0, 2)], xp)
        yield
        c["b"].wait_recv()
        part[j][pl.ds(((x + 3) % 4) * 4 + 2, 2)] += rx1[j][1]
        c["f"] = send(blocks(x + 3, 2, 2), rx2[j].at[1, pl.ds(2, 2)], xm)
        yield
        for name in ("c", "d", "e", "f"):
            c[name].wait_recv()
        part[j][pl.ds(x * 4, 4)] += rx2[j][0] + rx2[j][1]
        c["g"] = send(piece(zh + 2, 0, half), rz1[j].at[0, pl.ds(0, half)], zp)
        c["h"] = send(piece(zh + 2, half, rest), rz1[j].at[1, pl.ds(0, rest)], zm)
        c["i"] = send(piece(zh + 1, half, rest), rz2[j].at[0, pl.ds(half, rest)], zp)
        c["k"] = send(piece(zh + 3, 0, half), rz2[j].at[1, pl.ds(0, half)], zm)
        yield
        c["g"].wait_recv()
        part[j][x * 4 + (zh + 1) % 4, pl.ds(0, half)] += rz1[j][0, pl.ds(0, half)]
        c["l"] = send(piece(zh + 1, 0, half), rz2[j].at[0, pl.ds(0, half)], zp)
        yield
        c["h"].wait_recv()
        part[j][x * 4 + (zh + 3) % 4, pl.ds(half, rest)] += rz1[j][1, pl.ds(0, rest)]
        c["m"] = send(piece(zh + 3, half, rest), rz2[j].at[1, pl.ds(half, rest)], zm)
        yield
        for name in ("i", "k", "l", "m"):
            c[name].wait_recv()
        total = part[j][x * 4 + zh] + rz2[j][0] + rz2[j][1]
        rows = mine[j][...]
        slope = normal_cdf(rows) + rows * density(rows)
        pg[j][pl.ds(pl.multiple_of(col * bp, bp), bp)] = total * slope
        yield

    def pg_block(j):
        bp = chunks[j] * TILE

        def block(xx, hh, start, count):
            first = pl.multiple_of((xx * 4 + hh) * bp + start, TILE)
            return pg[j].at[pl.ds(first, count)]

        return block

    def p_block(ref, per_block, offset):
        def block(xx, hh, start, count):
            return ref.at[pl.ds((xx * 4 + hh) * per_block + offset + start, count)]

        return block

    def tables():
        live = [
            jnp.clip((kept_ref[b // 2] + (TILE - 1)) // TILE - b % 2 * OWN, 0, OWN)
            for b in range(HALVES)
        ]
        kept_here = [jnp.minimum(n, slots) for n in live]
        over = [n - k for n, k in zip(live, kept_here)]
        over_end = cumulative(over)
        free_end = cumulative([slots - k for k in kept_here])
        for b in range(HALVES):
            counts[0, b] = live[b]
            counts[1, b] = kept_here[b]
            counts[2, b] = over_end[b] - over[b]
            counts[3, b] = free_end[b] - slots
        yield

        def fill_block(b, carry):
            here, free = counts[1, b], counts[3, b]
            for j, t in enumerate(chunks):

                def fill(i, carry, j=j, t=t):
                    k = first_slot[j] + i
                    at = -1
                    if spare:
                        e = free + k
                        moved = e + slots
                        for n in range(HALVES - 1):
                            moved = moved + jnp.where(e >= over_end[n], OWN - over[n], 0)
                        at = jnp.where(e < over_end[-1], moved, -1)
                    src[HALVES * first_slot[j] + b * t + i] = jnp.where(k < here, b * OWN + k, at)
                    return carry

                lax.fori_loop(0, t, fill, 0)
            return carry

        lax.fori_loop(0, HALVES // 2, fill_block, 0)
        yield
        lax.fori_loop(HALVES // 2, HALVES, fill_block, 0)
        yield

        def place_block(b, carry):
            here = counts[0, b]

            def stay(k, carry):
                inv[b * OWN + k] = jnp.where(k < here, b * slots + k, -1)
                return carry

            lax.fori_loop(0, slots, stay, 0)
            if spare:
                begin = counts[2, b]

                def leave(i, carry):
                    e = begin + i
                    slot = e + kept_here[0]
                    for n in range(HALVES - 1):
                        slot = slot + jnp.where(e >= free_end[n], kept_here[n + 1], 0)
                    inv[b * OWN + slots + i] = jnp.where(slots + i < here, slot, -1)
                    return carry

                lax.fori_loop(0, spare, leave, 0)
            return carry

        lax.fori_loop(0, HALVES, place_block, 0)
        yield

    strips = slots // 2

    def fetch(ref, strip, masked):
        width = ref.shape[-1]

        def one(i, carry):
            at = src[strip * SAMPLE_TILES + i]
            tile = ref[jnp.maximum(at, 0)]
            if masked:
                tile = jnp.where(at >= 0, tile, 0.0)
            stage[pl.ds(pl.multiple_of(i * TILE, TILE), TILE), pl.ds(0, width)] = tile
            return carry

        lax.fori_loop(0, SAMPLE_TILES, one, 0, unroll=4)
        return stage[:, pl.ds(0, width)]

    def moved_tile(at, tile):
        if not spare:
            return tile
        at = jnp.maximum(at, 0)
        place = at % OWN - slots
        index = at // OWN * spare + jnp.maximum(place, 0)
        return jnp.where(place >= 0, p_over[index], tile)

    def fetch_p(strip, j):
        def one(i, carry):
            n = (strip - first_slot[j] // 2) * SAMPLE_TILES + i
            own = p_main[n // chunks[j] * slots + first_slot[j] + n % chunks[j]]
            at = src[strip * SAMPLE_TILES + i]
            stage[pl.ds(pl.multiple_of(i * TILE, TILE), TILE)] = moved_tile(at, own)
            return carry

        lax.fori_loop(0, SAMPLE_TILES, one, 0, unroll=4)

    def own_rows():
        for j, t in enumerate(chunks):

            def one(i, carry, j=j, t=t):
                at = src[HALVES * first_slot[j] + col * t + i]
                mine[j][pl.ds(pl.multiple_of(i * TILE, TILE), TILE)] = moved_tile(
                    at, p_ref[first_slot[j] + i]
                )
                return carry

            lax.fori_loop(0, t, one, 0)
        yield

    def pack_g():
        def body(strip, carry):
            span = pl.ds(pl.multiple_of(strip * PAD, PAD), PAD)
            gp_hi[span], gp_lo[span] = split(fetch(g_all, strip, True))
            return carry

        lax.fori_loop(0, strips, body, 0)
        yield

    def transposed(ref, to_hi, to_lo, masked):
        def body(strip, carry):
            high, low = split(fetch(ref, strip, masked).T)
            to_hi[strip] = high
            to_lo[strip] = low
            return carry

        lax.fori_loop(0, strips // 2, body, 0)
        yield
        lax.fori_loop(strips // 2, strips, body, 0)
        yield

    def w_out_split():
        weights[0].wait()

        def body(n, carry):
            rows = pl.ds(pl.multiple_of(n * LC, LC), LC)
            wout_hi[n], wout_lo[n] = split(wout_f[rows].T)
            return carry

        lax.fori_loop(0, LANES, body, 0)
        yield

    def w_in_split():
        weights[1].wait()

        def body(n, carry):
            win_hi[n], win_lo[n] = split(win_f[:, lanes(n)].T)
            return carry

        lax.fori_loop(0, LANES, body, 0)
        yield

    def w_out_grad():
        dwt[...] = jnp.zeros_like(dwt)
        for j, t in enumerate(chunks):

            def body(strip, carry, j=j):
                fetch_p(strip, j)
                left = gt_hi[strip], gt_lo[strip]

                def step(n, carry):
                    value = stage[:, lanes(n)]
                    dwt[n] += product(left, split(value * normal_cdf(value)))
                    return carry

                return lax.fori_loop(0, LANES, step, carry)

            lax.fori_loop(first_slot[j] // 2, (first_slot[j] + t) // 2, body, 0)
            yield

    def w_out_last():
        def body(n, carry):
            dwout_ref[pl.ds(pl.multiple_of(n * LC, LC), LC)] = dwt[n].T
            return carry

        lax.fori_loop(0, LANES, body, 0)
        yield

    def w_in_grad(j):
        if j == 0:
            dwin_ref[...] = jnp.zeros_like(dwin_ref)

        def body(i, carry):
            strip = first_slot[j] // 2 + i
            span = pl.ds(pl.multiple_of(i * PAD, PAD), PAD)
            left = xt_hi[strip], xt_lo[strip]

            def step(n, carry):
                dwin_ref[:, lanes(n)] += product(left, split(pg[j][span, lanes(n)]))
                return carry

            return lax.fori_loop(0, LANES, step, carry)

        lax.fori_loop(0, chunks[j] // 2, body, 0)
        yield

    def x_grad(j):
        t = chunks[j]

        def body(i, carry):
            span = pl.ds(pl.multiple_of(i * PAD, PAD), PAD)
            acc[...] = jnp.zeros_like(acc)

            def step(n, carry):
                left = split(pg[j][span, lanes(n)])
                acc[...] += product(left, (win_hi[n], win_lo[n])).reshape(acc.shape)
                return carry

            lax.fori_loop(0, LANES, step, carry)

            def place(q, carry):
                tile = i * SAMPLE_TILES + q
                dxp[tile // t * slots + first_slot[j] + tile % t] = acc[q]
                return carry

            return lax.fori_loop(0, SAMPLE_TILES, place, carry, unroll=4)

        lax.fori_loop(0, t // 2, body, 0)
        yield

    def row_sum(n, low, high):
        size = high - low

        def spread(yy, cc):
            yy = yy % 4

            def one(i, carry):
                ll, k = i // size, i % size
                at = inv[(yy * 4 + ll * 2 + cc) * OWN + low + k]
                tile = dxp[jnp.maximum(at, 0)]
                dxs[n][cc, yy, i] = jnp.where(at >= 0, tile, 0.0)
                return carry

            lax.fori_loop(0, 2 * size, one, 0, unroll=2)

        order = (y + 2, y + 1, y + 3, y)
        s = []
        for k, yy in enumerate(order):
            spread(yy, 1 - core)
            s.append(send(dxs[n].at[1 - core, yy % 4], dsib[n].at[k], sib))
        yield
        for yy in order:
            spread(yy, core)

        def blocks(yy, ll):
            return dxs[n].at[core, yy % 4, pl.ds(ll * size, size)]

        def add_sib(k):
            s[k].wait_recv()
            dxs[n][core, order[k] % 4] += dsib[n][k]

        yield
        c = {}
        add_sib(0)
        c["a"] = send(blocks(y + 2, 0), dy1[n].at[0], yp)
        c["b"] = send(blocks(y + 2, 1), dy1[n].at[1], ym)
        yield
        add_sib(1)
        c["c"] = send(blocks(y + 1, 1), dy2[n].at[0, pl.ds(size, size)], yp)
        yield
        add_sib(2)
        c["d"] = send(blocks(y + 3, 0), dy2[n].at[1, pl.ds(0, size)], ym)
        yield
        add_sib(3)
        yield
        c["a"].wait_recv()
        dxs[n][core, (y + 1) % 4, pl.ds(0, size)] += dy1[n][0]
        c["e"] = send(blocks(y + 1, 0), dy2[n].at[0, pl.ds(0, size)], yp)
        yield
        c["b"].wait_recv()
        dxs[n][core, (y + 3) % 4, pl.ds(size, size)] += dy1[n][1]
        c["f"] = send(blocks(y + 3, 1), dy2[n].at[1, pl.ds(size, size)], ym)
        yield
        for name in ("c", "d", "e", "f"):
            c[name].wait_recv()
        dxs[n][core, y] += dy2[n][0] + dy2[n][1]
        c["z"] = send(blocks(y, 1 - zl), dz[n], zlp)
        yield
        c["z"].wait_recv()
        dx_ref[pl.ds(low, size)] = dxs[n][core, y, pl.ds(zl * size, size)] + dz[n][...]
        yield

    early = first_slot[-1]
    parts = {
        "g": row_gather(g_all),
        "x": row_gather(x_all),
        "p": col_gather(p_block(p_main, slots, cross), slots - cross),
        "q": col_gather(p_block(p_main, slots, 0), cross, z_first=False),
        "tab": tables(),
        "wo": w_out_split(),
        "wi": w_in_split(),
        "pack": pack_g(),
        "own": own_rows(),
        "gt": transposed(g_all, gt_hi, gt_lo, True),
        "xt": transposed(x_all, xt_hi, xt_lo, False),
        "dwo": w_out_grad(),
        "dwf": w_out_last(),
        "t0": row_sum(0, 0, early),
        "t1": row_sum(1, early, OWN),
    }
    if spare:
        parts["o"] = col_gather(p_block(p_over, spare, 0), spare)
    for j in range(len(chunks)):
        parts[f"s{j}"] = col_sum(j)
        parts[f"a{j}"] = col_gather(pg_block(j), chunks[j] * TILE)
        parts[f"dx{j}"] = x_grad(j)
        parts[f"dw{j}"] = w_in_grad(j)
    for name in ORDER if spare else ORDER_FULL:
        next(parts[name])
    for left in parts.values():
        assert next(left, None) is None
    for copy in started:
        copy.wait_send()
    assert len(started) <= COPIES


def grad_kernel(slots, out_grad, inputs, pre_act, w_in, w_out, kept):
    chunks, cross = PLANS[slots]
    spare = OWN - slots
    early = slots - chunks[-1]
    vmem = pl.BlockSpec(memory_space=pltpu.VMEM)
    anywhere = pl.BlockSpec(memory_space=pl.ANY)

    def room(*shape, dtype=F32):
        return pltpu.VMEM(shape, dtype)

    half = functools.partial(room, dtype=BF16)

    def each(make):
        return [make(t * TILE) for t in chunks]

    def both(make):
        return [make(early), make(OWN - early)]

    dx, dwin, dwout = pl.pallas_call(
        functools.partial(kernel, slots, chunks, cross),
        out_shape=(
            jax.ShapeDtypeStruct((OWN, TILE, D), F32),
            jax.ShapeDtypeStruct((D, F), F32),
            jax.ShapeDtypeStruct((F, D), F32),
        ),
        in_specs=[pl.BlockSpec(memory_space=pltpu.SMEM), vmem, vmem, vmem, anywhere, anywhere],
        out_specs=(vmem, vmem, vmem),
        scratch_shapes=[
            pltpu.SMEM((HALVES * slots,), jnp.int32),
            pltpu.SMEM((TILES,), jnp.int32),
            room(TILES, TILE, D),
            room(TILES, TILE, D),
            room(HALVES * slots, TILE, F),
            room(max(HALVES * spare, 1), TILE, F),
            each(lambda r: room(HALVES, r, F)),
            each(lambda r: room(2, 2, r, F)),
            each(lambda r: room(2, 4, r, F)),
            each(lambda r: room(2, r - r // 16 * TILE, F)),
            each(lambda r: room(2, r, F)),
            each(lambda r: room(HALVES * r, F)),
            half(HALVES * slots * TILE, D),
            half(HALVES * slots * TILE, D),
            half(slots // 2, D, PAD),
            half(slots // 2, D, PAD),
            half(slots // 2, D, PAD),
            half(slots // 2, D, PAD),
            room(D, F),
            room(F, D),
            half(LANES, LC, D),
            half(LANES, LC, D),
            half(LANES, D, LC),
            half(LANES, D, LC),
            room(HALVES * slots, TILE, D),
            both(lambda e: room(2, 4, 2 * e, TILE, D)),
            both(lambda e: room(4, 2 * e, TILE, D)),
            both(lambda e: room(2, e, TILE, D)),
            both(lambda e: room(2, 2 * e, TILE, D)),
            both(lambda e: room(e, TILE, D)),
            room(LANES, D, LC),
            room(SAMPLE_TILES, TILE, D),
            room(PAD, F),
            each(lambda r: room(r, F)),
            pltpu.SMEM((4, HALVES), jnp.int32),
            pltpu.SemaphoreType.DMA((COPIES,)),
            pltpu.SemaphoreType.DMA((COPIES,)),
            pltpu.SemaphoreType.DMA((2,)),
        ],
        compiler_params=pltpu.CompilerParams(
            collective_id=slots, has_side_effects=True, vmem_limit_bytes=64 * 1024 * 1024
        ),
        cost_estimate=pl.CostEstimate(flops=24 * slots * ROWS * D * F, bytes_accessed=6 * 1024 * 1024, transcendentals=0),
    )(
        kept,
        out_grad.reshape(OWN, TILE, D),
        inputs.reshape(OWN, TILE, D),
        pre_act.reshape(OWN, TILE, F),
        w_in,
        w_out,
    )
    return dx.reshape(ROWS, D), dwin, dwout


def settle_kernel(*refs):
    sources, targets, rooms, sems = refs[:3], refs[3:6], refs[6:9], refs[9]
    pieces = []
    for source, target, space in zip(sources, targets, rooms):
        rows = source.shape[0] // 2
        pieces += [
            tuple(ref.at[pl.ds(k * rows, rows)] for ref in (source, space, target)) for k in range(2)
        ]
    inward = [
        pltpu.make_async_copy(a, b, sems.at[0, k]) for k, (a, b, _) in enumerate(pieces)
    ]
    outward = [
        pltpu.make_async_copy(b, c, sems.at[1, k]) for k, (_, b, c) in enumerate(pieces)
    ]
    for copy in inward:
        copy.start()
    for first, second in zip(inward, outward):
        first.wait()
        second.start()
    for copy in outward:
        copy.wait()


def settle(*arrays):
    anywhere = pl.BlockSpec(memory_space=pl.ANY)
    return pl.pallas_call(
        settle_kernel,
        out_shape=tuple(jax.ShapeDtypeStruct(a.shape, a.dtype) for a in arrays),
        in_specs=[anywhere] * 3,
        out_specs=(anywhere,) * 3,
        scratch_shapes=[pltpu.VMEM(a.shape, a.dtype) for a in arrays]
        + [pltpu.SemaphoreType.DMA((2, 6))],
        compiler_params=pltpu.CompilerParams(vmem_limit_bytes=60 * 1024 * 1024),
    )(*arrays)


def shards(*args):
    tiles = jnp.sum((args[-1] + (TILE - 1)) // TILE)
    choices = sorted(PLANS)
    index = sum((tiles > HALVES * slots).astype(jnp.int32) for slots in choices[:-1])
    grads = lax.switch(index, [functools.partial(grad_kernel, slots) for slots in choices], *args)
    return settle(*grads)


def solution(mesh):
    return jax.shard_map(
        shards,
        mesh=mesh,
        in_specs=(
            P("row", "col"),
            P("row", "col"),
            P("col", "row"),
            P("col", "row"),
            P("row", "col"),
            P(),
        ),
        out_specs=(P("row", "col"), P("col", "row"), P("row", "col")),
        check_vma=False,
    )
```
